32 devices in a mesh: seq: 2 (over y), fsdp: 16 (over z, x, core).
Axes of the slice: x: 2, y: 2, z: 4, core: 2. Of those that a mesh axis runs over, the one named last changes fastest.
Arguments:
- token_ids: int32 [16, 2048], P('fsdp', 'seq'), may hold values from 0 to 151935
- seq_lengths: int32 [16, 4], P('fsdp'), may hold values from 1 to 1024, 2048 in all within a row
- pairing: int32 [48], replicated, may hold values from 0 to 47, each once
- step_count: float32 [1], replicated, may hold values from 1 to 20
- embedding: float32 [151936, 1024], P('fsdp', 'seq'), may hold values from -0.6 to 0.6
- embedding_one: float32 [151936, 1024], P('fsdp', 'seq'), may hold values from -5e-05 to 5e-05
- embedding_two: float32 [151936, 1024], P('fsdp', 'seq'), may hold values from 3e-10 to 1.2e-09
- qkv_weight: float32 [1024, 4096], P(('seq', 'fsdp')), may hold values from -0.1875 to 0.1875
- qkv_one: float32 [1024, 4096], P(('seq', 'fsdp')), may hold values from -0.00015 to 0.00015
- qkv_two: float32 [1024, 4096], P(('seq', 'fsdp')), may hold values from 2.8e-09 to 1.1e-08
- out_weight: float32 [2048, 1024], P(('seq', 'fsdp')), may hold values from -1 to 1
- out_one: float32 [2048, 1024], P(('seq', 'fsdp')), may hold values from -0.00015 to 0.00015
- out_two: float32 [2048, 1024], P(('seq', 'fsdp')), may hold values from 2.8e-09 to 1.1e-08
- gate_up_weight: float32 [1024, 6144], P(('seq', 'fsdp')), may hold values from -0.1875 to 0.1875
- gate_up_one: float32 [1024, 6144], P(('seq', 'fsdp')), may hold values from -0.00015 to 0.00015
- gate_up_two: float32 [1024, 6144], P(('seq', 'fsdp')), may hold values from 2.8e-09 to 1.1e-08
- down_weight: float32 [3072, 1024], P(('seq', 'fsdp')), may hold values from -0.109375 to 0.109375
- down_one: float32 [3072, 1024], P(('seq', 'fsdp')), may hold values from -0.00015 to 0.00015
- down_two: float32 [3072, 1024], P(('seq', 'fsdp')), may hold values from 2.8e-09 to 1.1e-08
- norm_gains: float32 [3328], replicated, may hold values from 0.5 to 1.5
- gains_one: float32 [3328], replicated, may hold values from -0.00033 to 0.00033
- gains_two: float32 [3328], replicated, may hold values from 1e-08 to 4e-08
- score_weight: float32 [1024], replicated, may hold values from -0.1875 to 0.1875
- score_one: float32 [1024], replicated, may hold values from -0.0066 to 0.0066
- score_two: float32 [1024], replicated, may hold values from 5.3e-06 to 2.1e-05
Outputs:
- ranking_loss: float32 [], replicated
- grad_norm: float32 [], replicated
- new_embedding: float32 [151936, 1024], P('fsdp', 'seq')
- new_embedding_one: float32 [151936, 1024], P('fsdp', 'seq')
- new_embedding_two: float32 [151936, 1024], P('fsdp', 'seq')
- new_qkv: float32 [1024, 4096], P(('seq', 'fsdp'))
- new_qkv_one: float32 [1024, 4096], P(('seq', 'fsdp'))
- new_qkv_two: float32 [1024, 4096], P(('seq', 'fsdp'))
- new_out: float32 [2048, 1024], P(('seq', 'fsdp'))
- new_out_one: float32 [2048, 1024], P(('seq', 'fsdp'))
- new_out_two: float32 [2048, 1024], P(('seq', 'fsdp'))
- new_gate_up: float32 [1024, 6144], P(('seq', 'fsdp'))
- new_gate_up_one: float32 [1024, 6144], P(('seq', 'fsdp'))
- new_gate_up_two: float32 [1024, 6144], P(('seq', 'fsdp'))
- new_down: float32 [3072, 1024], P(('seq', 'fsdp'))
- new_down_one: float32 [3072, 1024], P(('seq', 'fsdp'))
- new_down_two: float32 [3072, 1024], P(('seq', 'fsdp'))
- clipped_gains: float32 [3328], replicated
- new_gains_one: float32 [3328], replicated
- new_gains_two: float32 [3328], replicated
- new_score: float32 [1024], replicated
- new_score_one: float32 [1024], replicated
- new_score_two: float32 [1024], replicated
The draws below stay inside these ranges and needn't reach their ends.
Inputs may be any that keep to these rules, and one draw needn't show every extreme that they name: `token_ids`: the ids of padding tokens are drawn like the others. `seq_lengths`: each row holds the lengths of its group's 4 - 1 sequences in token order, then the padding's length; a row sums to 2048 and its largest entry is 1024. A permutation of the 48 sequence numbers; pair p prefers sequence pairing[2p] to pairing[2p + 1].
All inputs are finite; a program needn't handle non-finite values.
Results may differ from the reference program's by a relative error of at most 0.012.
Values may be sent and summed in bfloat16 or wider, within the bound.
A program may use at most 352 MiB of HBM per device.

```python
import math
import jax
import jax.numpy as jnp
import numpy as np
from jax import lax

D = 1024
QUERY_HEADS = 16
KEY_VALUE_HEADS = 8
HEAD_SIZE = 128
FF = 3072
V = 151936
SLOTS = 4
GROUPS = 16
GROUP_TOKENS = 2048
MOST_LEN = 1024
NSEQS = 48
NPAIRS = 24
BLOCK = 512
QKV = 4096
GAINS = 3328


def place_ends(array, own_key, low, high):
    shape = array.shape
    index_at = [jax.random.randint(jax.random.fold_in(own_key, axis), (), 0, shape[axis]) for axis in range(len(shape))]
    array = array.at[tuple(index_at)].set(low)
    longest = shape.index(max(shape))
    index_at[longest] = (index_at[longest] + 1) % shape[longest]
    return array.at[tuple(index_at)].set(high)


def shard_levels(rng, shape, cuts, low, largest):
    def one(dim, parts):
        steps = jax.random.uniform(jax.random.fold_in(jax.random.fold_in(rng, 6), dim), (parts,), jnp.float32, low / len(cuts), largest / len(cuts))
        return jnp.repeat(jnp.exp(steps), shape[dim] // parts).reshape((-1,) + (1,) * (len(shape) - dim - 1))

    loudness = one(*cuts[0])
    for cut in cuts[1:]:
        loudness = loudness * one(*cut)
    return loudness


def wide_ids(own_key, extent, number_of, lean):
    portions = [min(1 << octave, number_of + 1 - (1 << octave)) * (1 << 20) // math.isqrt((1 << octave) ** lean) + 1 for octave in range((number_of + 1).bit_length()) if 1 << octave <= number_of]
    width = 1 + sum(portions) // (1 << 30)
    grid = np.cumsum(np.array([max(1, weight // width) for weight in portions]))
    pick = jax.random.randint(jax.random.fold_in(own_key, 1), extent, 0, int(grid[len(portions) - 1]))
    start = jnp.left_shift(1, jnp.searchsorted(jnp.asarray(grid, jnp.int32), pick, side="right").astype(jnp.int32))
    grade = start - 1 + jax.random.randint(jax.random.fold_in(own_key, 4), extent, 0, 1 << 30) % jnp.minimum(start, number_of + 1 - start)
    return jax.random.permutation(jax.random.fold_in(own_key, 2), number_of)[grade].astype(jnp.int32)


def profile(number_of, total, bound, slope):
    portions = [(1 << 20) // math.isqrt(grade ** slope) + 1 for grade in range(2, number_of + 1)]
    rest, holding = total - bound - (number_of - 1), [1] * (number_of - 1)
    while rest > 0:
        free = [i for i in range(number_of - 1) if holding[i] < bound]
        pool, budget = sum([portions[i] for i in free]), rest
        for i in free:
            addition = min(bound - holding[i], max(1, budget * portions[i] // pool), rest)
            holding[i] = holding[i] + addition
            rest = rest - addition
    return np.array([bound] + holding)


def uneven_parts(own_key, amount, total, bound, lean):
    if amount == 2:
        one = jax.random.randint(own_key, (), max(1, total - bound), min(bound, total - 1) + 1)
        return jnp.stack([one, total - one])
    tallies = jnp.asarray(profile(amount, total, bound, lean), jnp.int32)
    pairs = (amount - 1) // 2
    source_of, receiver = tallies[1:1 + 2 * pairs:2], tallies[2:2 + 2 * pairs:2]
    slack = jnp.minimum(source_of - 1, bound - receiver)
    passed = jax.random.randint(jax.random.fold_in(own_key, 1), (pairs,), 0, 1 << 20) % (slack + 1)
    tallies = tallies.at[1:1 + 2 * pairs:2].set(source_of - passed).at[2:2 + 2 * pairs:2].set(receiver + passed)
    return tallies[jax.random.permutation(jax.random.fold_in(own_key, 2), amount)]


def normal_values(stream_key, dims, width, limit, cuts=(), kind=jnp.bfloat16):
    array = jax.random.normal(stream_key, dims, jnp.float32) * width
    if len(cuts) > 0:
        array = shard_levels(stream_key, dims, cuts, -0.22, 0.18) * array
    return jnp.clip(array, min=-limit, max=limit).astype(kind)


def setup_inputs(seed: int = 0) -> dict:
    key_list = jax.random.split(jax.random.key(seed), 26)
    token_ids = place_ends(wide_ids(key_list[0], (GROUPS, GROUP_TOKENS), V, 2), jax.random.fold_in(key_list[0], 3), 0, V - 1).astype(jnp.int32)
    seq_lengths = jax.vmap(lambda own: uneven_parts(own, SLOTS, GROUP_TOKENS, MOST_LEN, 2))(jax.random.split(key_list[1], GROUPS)).reshape((GROUPS, SLOTS)).astype(jnp.int32)
    pairing = jax.random.permutation(key_list[2], NSEQS).astype(jnp.int32)
    step_count = jnp.clip(jax.random.uniform(key_list[3], (1,), jnp.float32, 1.0, 20.0), 1.0, 20.0)
    embedding = normal_values(key_list[4], (V, D), 0.1, 0.6, ((0, 16), (1, 2)), jnp.float32)
    embedding_one = normal_values(key_list[5], (V, D), 0.0000084, 4.999999873689376e-05, ((0, 16), (1, 2)), jnp.float32)
    embedding_two = jnp.clip(jnp.exp(math.log(1.1999999882661427e-09) - 1.3862944 * jax.random.uniform(key_list[6], (V, D), jnp.float32) ** shard_levels(key_list[6], (V, D), ((0, 16), (1, 2)), -0.2, 0.2)), 2.999999970665357e-10, 1.1999999882661427e-09)
    qkv_weight = normal_values(key_list[7], (D, QKV), D ** -0.5, 0.1875, ((0, 32),), jnp.float32)
    qkv_one = normal_values(key_list[8], (D, QKV), 0.000025, 0.00015, ((0, 32),), jnp.float32)
    qkv_two = jnp.clip(jnp.exp(math.log(1.1000000021965661e-08) - 1.3682759 * jax.random.uniform(key_list[9], (D, QKV), jnp.float32) ** shard_levels(key_list[9], (D, QKV), ((0, 32),), -0.2, 0.2)), 2.800000009628434e-09, 1.1000000021965661e-08)
    out_weight = normal_values(key_list[10], (QUERY_HEADS * HEAD_SIZE, D), (QUERY_HEADS * HEAD_SIZE // 64) ** -0.5, 1.0, ((0, 32),), jnp.float32)
    out_one = normal_values(key_list[11], (QUERY_HEADS * HEAD_SIZE, D), 0.000025, 0.00015, ((0, 32),), jnp.float32)
    out_two = jnp.clip(jnp.exp(math.log(1.1000000021965661e-08) - 1.3682759 * jax.random.uniform(key_list[12], (QUERY_HEADS * HEAD_SIZE, D), jnp.float32) ** shard_levels(key_list[12], (QUERY_HEADS * HEAD_SIZE, D), ((0, 32),), -0.2, 0.2)), 2.800000009628434e-09, 1.1000000021965661e-08)
    gate_up_weight = normal_values(key_list[13], (D, 2 * FF), D ** -0.5, 0.1875, ((0, 32),), jnp.float32)
    gate_up_one = normal_values(key_list[14], (D, 2 * FF), 0.000025, 0.00015, ((0, 32),), jnp.float32)
    gate_up_two = jnp.clip(jnp.exp(math.log(1.1000000021965661e-08) - 1.3682759 * jax.random.uniform(key_list[15], (D, 2 * FF), jnp.float32) ** shard_levels(key_list[15], (D, 2 * FF), ((0, 32),), -0.2, 0.2)), 2.800000009628434e-09, 1.1000000021965661e-08)
    down_weight = normal_values(key_list[16], (FF, D), FF ** -0.5, 0.109375, ((0, 32),), jnp.float32)
    down_one = normal_values(key_list[17], (FF, D), 0.000025, 0.00015, ((0, 32),), jnp.float32)
    down_two = jnp.clip(jnp.exp(math.log(1.1000000021965661e-08) - 1.3682759 * jax.random.uniform(key_list[18], (FF, D), jnp.float32) ** shard_levels(key_list[18], (FF, D), ((0, 32),), -0.2, 0.2)), 2.800000009628434e-09, 1.1000000021965661e-08)
    norm_gains = jnp.clip(1.0 + 0.1 * jax.random.normal(key_list[19], (GAINS,), jnp.float32), 0.5, 1.5)
    gains_one = normal_values(key_list[20], (GAINS,), 0.000055, 0.00033, (), jnp.float32)
    gains_two = jnp.clip(jnp.exp(jax.random.uniform(key_list[21], (GAINS,), jnp.float32, math.log(9.99999993922529e-09), math.log(3.999999975690116e-08))), 9.99999993922529e-09, 3.999999975690116e-08)
    score_weight = normal_values(key_list[22], (D,), D ** -0.5, 0.1875, (), jnp.float32)
    score_one = normal_values(key_list[23], (D,), 0.0011, 0.0066, (), jnp.float32)
    score_two = jnp.clip(jnp.exp(jax.random.uniform(key_list[24], (D,), jnp.float32, math.log(5.299999884300632e-06), math.log(2.099999983329326e-05))), 5.299999884300632e-06, 2.099999983329326e-05)
    return {"token_ids": token_ids, "seq_lengths": seq_lengths, "pairing": pairing, "step_count": step_count, "embedding": embedding, "embedding_one": embedding_one, "embedding_two": embedding_two, "qkv_weight": qkv_weight, "qkv_one": qkv_one, "qkv_two": qkv_two, "out_weight": out_weight, "out_one": out_one, "out_two": out_two, "gate_up_weight": gate_up_weight, "gate_up_one": gate_up_one, "gate_up_two": gate_up_two, "down_weight": down_weight, "down_one": down_one, "down_two": down_two, "norm_gains": norm_gains, "gains_one": gains_one, "gains_two": gains_two, "score_weight": score_weight, "score_one": score_one, "score_two": score_two}


NORM_EPS = 1e-06
ROPE_THETA = 1000000.0
LEARN_RATE = 0.04
BETA_ONE = 0.9
BETA_TWO = 0.95
ADAM_EPS = 1e-08
WEIGHT_DECAY = 0.1
CLIP_NORM = 1.0
PRECISE = lax.Precision.HIGHEST
MASKED = -1e+30

@jax.custom_vjp
def low(v):
    return lax.optimization_barrier(v.astype(jnp.bfloat16)).astype(jnp.float32)

@jax.custom_vjp
def low_back(v):
    return v

def low_keep(v):
    return (low(v), None)

def low_pass(kept, grad):
    return (grad,)

def back_keep(v):
    return (v, None)

def back_low(kept, grad):
    return (low(grad),)
low.defvjp(low_keep, low_pass)
low_back.defvjp(back_keep, back_low)

def rms_norm(values, gain_vec):
    return values * lax.rsqrt(lax.optimization_barrier(jnp.mean(values * values, axis=-1, keepdims=True)) + NORM_EPS) * gain_vec

def rotary(values, position):
    half_width = values.shape[-1] // 2
    frequency = ROPE_THETA ** (-2.0 * jnp.arange(half_width, dtype=jnp.float32) / values.shape[-1])
    angles = position.astype(jnp.float32)[:, None] * frequency[None, :]
    cosine = jnp.cos(angles)[:, None, :]
    sine_part = jnp.sin(angles)[:, None, :]
    lower = values[..., :half_width]
    upper = values[..., half_width:]
    return jnp.concatenate([lower * cosine - upper * sine_part, upper * cosine + lower * sine_part], axis=-1)

def layout(seg_ends, length):
    token_pos = jnp.arange(length, dtype=jnp.int32)
    bounds = seg_ends[:-1]
    segment = lax.optimization_barrier(jnp.sum((token_pos[:, None] >= bounds[None, :]).astype(jnp.int32), axis=1)).astype(jnp.int32)
    starts_all = jnp.concatenate([jnp.zeros((1,), jnp.int32), bounds])
    slot_ids = jnp.arange(seg_ends.shape[0], dtype=jnp.int32)
    begin = lax.optimization_barrier(jnp.sum(jnp.where(segment[:, None] == slot_ids[None, :], starts_all[None, :], 0), axis=1)).astype(jnp.int32)
    return (segment, token_pos - begin)

def masked(scores, row_start, block_size, segment):
    key_pos = jnp.arange(segment.shape[0], dtype=jnp.int32)
    row_pos = row_start + jnp.arange(block_size, dtype=jnp.int32)
    row_seg = lax.dynamic_slice_in_dim(segment, row_start, block_size)
    allowed = (key_pos[None, :] <= row_pos[:, None]) & (segment[None, :] == row_seg[:, None])
    return jnp.where(allowed[None], scores, MASKED)

def attend(query_low, key_low, value_low, segment):
    group_length = QUERY_HEADS // KEY_VALUE_HEADS
    key_all = jnp.repeat(key_low, group_length, axis=1)
    value_all = jnp.repeat(value_low, group_length, axis=1)

    def one_block(row_start):
        row_block = lax.dynamic_slice_in_dim(query_low, row_start, BLOCK)
        scores = jnp.einsum('qhd,khd->hqk', row_block, key_all, precision=PRECISE) * HEAD_SIZE ** (-0.5)
        scores = masked(low_back(scores), row_start, BLOCK, segment)
        probs = low(jax.nn.softmax(scores, axis=-1))
        return jnp.einsum('hqk,khd->qhd', probs, value_all, precision=PRECISE)
    starts = jnp.arange(GROUP_TOKENS // BLOCK, dtype=jnp.int32) * BLOCK
    output = lax.map(jax.checkpoint(one_block), starts)
    return output.reshape(GROUP_TOKENS, QUERY_HEADS, HEAD_SIZE)

def group_scores(resid_in, seg_ends, qkv_w, out_w, gate_up_w, down_w, gains_w, score_w):
    attn_gain = gains_w[:D]
    mlp_gain = gains_w[D:2 * D]
    final_gain = gains_w[2 * D:3 * D]
    query_gain = gains_w[3 * D:3 * D + HEAD_SIZE]
    key_gain = gains_w[3 * D + HEAD_SIZE:]
    segment, position = layout(seg_ends, GROUP_TOKENS)
    normed = low(rms_norm(resid_in, attn_gain))
    projected_rows = low(low_back(jnp.dot(normed, qkv_w, precision=PRECISE)))
    queries = projected_rows[:, :QUERY_HEADS * HEAD_SIZE].reshape(GROUP_TOKENS, QUERY_HEADS, HEAD_SIZE)
    key_head_rows = projected_rows[:, QUERY_HEADS * HEAD_SIZE:(QUERY_HEADS + KEY_VALUE_HEADS) * HEAD_SIZE].reshape(GROUP_TOKENS, KEY_VALUE_HEADS, HEAD_SIZE)
    value_head_rows = projected_rows[:, (QUERY_HEADS + KEY_VALUE_HEADS) * HEAD_SIZE:].reshape(GROUP_TOKENS, KEY_VALUE_HEADS, HEAD_SIZE)
    query_low = low(rotary(rms_norm(queries, query_gain), position))
    key_low = low(rotary(rms_norm(key_head_rows, key_gain), position))
    attended = attend(query_low, key_low, value_head_rows, segment)
    merged = low(low_back(attended)).reshape(GROUP_TOKENS, QUERY_HEADS * HEAD_SIZE)
    resid_mid = resid_in + low_back(jnp.dot(merged, out_w, precision=PRECISE))
    normed_two = low(rms_norm(resid_mid, mlp_gain))
    gate_up = low_back(jnp.dot(normed_two, gate_up_w, precision=PRECISE))
    activated = low(jax.nn.silu(gate_up[:, :FF]) * gate_up[:, FF:])
    resid_out = resid_mid + low_back(jnp.dot(activated, down_w, precision=PRECISE))
    final = rms_norm(resid_out, final_gain)
    per_token = jnp.dot(final, score_w, precision=PRECISE)
    slot_list = jnp.arange(SLOTS - 1, dtype=jnp.int32)
    member = (segment[None, :] == slot_list[:, None]).astype(jnp.float32)
    seq_begin = jnp.concatenate([jnp.zeros((1,), jnp.int32), seg_ends[:SLOTS - 2]])
    seq_size = (seg_ends[:SLOTS - 1] - seq_begin).astype(jnp.float32)
    return jnp.dot(member, per_token, precision=PRECISE) / seq_size

def adam_update(weight, moment_one, moment_two, grad, factor, step_float):
    grad = grad * factor
    moment_one = BETA_ONE * moment_one + (1.0 - BETA_ONE) * grad
    moment_two = BETA_TWO * moment_two + (1.0 - BETA_TWO) * grad * grad
    fix_one = 1.0 - BETA_ONE ** step_float
    fix_two = 1.0 - BETA_TWO ** step_float
    weight = weight - LEARN_RATE * (moment_one / fix_one / (jnp.sqrt(moment_two / fix_two) + ADAM_EPS) + WEIGHT_DECAY * weight)
    return (weight, moment_one, moment_two)

def reference(token_ids, seq_lengths, pairing, step_count, embedding, embedding_one, embedding_two, qkv_weight, qkv_one, qkv_two, out_weight, out_one, out_two, gate_up_weight, gate_up_one, gate_up_two, down_weight, down_one, down_two, norm_gains, gains_one, gains_two, score_weight, score_one, score_two):
    seg_ends = jnp.cumsum(seq_lengths, axis=1).astype(jnp.int32)
    pair_table = pairing.reshape(NPAIRS, 2)

    def total_loss(embed_w, qkv_w, out_w, gate_up_w, down_w, gains_w, score_w):
        resid = low_back(low(embed_w)[token_ids])
        lowered = (low(qkv_w), low(out_w), low(gate_up_w), low(down_w))

        def one_group(packed):
            return jax.checkpoint(group_scores)(packed[0], packed[1], *lowered, gains_w, score_w)
        scores = lax.map(one_group, (resid, seg_ends)).reshape(-1)
        margin = scores[pair_table[:, 0]] - scores[pair_table[:, 1]]
        return jnp.sum(jax.nn.softplus(-margin))
    ranking_loss, back_fn = jax.vjp(total_loss, embedding, qkv_weight, out_weight, gate_up_weight, down_weight, norm_gains, score_weight)
    gradients = back_fn(jnp.ones_like(ranking_loss))
    square = jnp.zeros((), jnp.float32)
    for grad in gradients:
        square = square + jnp.sum(grad * grad)
    grad_norm = jnp.sqrt(square)
    factor = CLIP_NORM / jnp.maximum(grad_norm, CLIP_NORM)
    step_float = step_count[0].astype(jnp.float32)
    e_new = adam_update(embedding, embedding_one, embedding_two, gradients[0], factor, step_float)
    q_new = adam_update(qkv_weight, qkv_one, qkv_two, gradients[1], factor, step_float)
    o_new = adam_update(out_weight, out_one, out_two, gradients[2], factor, step_float)
    g_new = adam_update(gate_up_weight, gate_up_one, gate_up_two, gradients[3], factor, step_float)
    d_new = adam_update(down_weight, down_one, down_two, gradients[4], factor, step_float)
    n_new = adam_update(norm_gains, gains_one, gains_two, gradients[5], factor, step_float)
    s_new = adam_update(score_weight, score_one, score_two, gradients[6], factor, step_float)
    clipped_gains = gradients[5] * factor
    return (ranking_loss, grad_norm, e_new[0], e_new[1], e_new[2], q_new[0], q_new[1], q_new[2], o_new[0], o_new[1], o_new[2], g_new[0], g_new[1], g_new[2], d_new[0], d_new[1], d_new[2], clipped_gains, n_new[1], n_new[2], s_new[0], s_new[1], s_new[2])
```

```python
import functools

import jax
import jax.numpy as jnp
from jax import lax
from jax.experimental import pallas as pl
from jax.experimental.pallas import tpu as pltpu
from jax.sharding import PartitionSpec as P

D = 1024
QUERY_HEADS = 16
KEY_VALUE_HEADS = 8
HEAD_SIZE = 128
FF = 3072
QUERY_COLS = QUERY_HEADS * HEAD_SIZE
KEY_COLS = KEY_VALUE_HEADS * HEAD_SIZE

NORM_EPS = 1e-06
ROPE_THETA = 1000000.0
LEARN_RATE = 0.04
BETA_ONE = 0.9
BETA_TWO = 0.95
ADAM_EPS = 1e-08
WEIGHT_DECAY = 0.1
CLIP_NORM = 1.0
PRECISE = lax.Precision.HIGHEST
MASKED = -1e30
LOG2E = 1.4426950408889634
MESH = pl.DeviceIdType.MESH
VMEM_BYTES = 56 * 2**20


def rms_norm(values, gain_vec):
    return (
        values * lax.rsqrt(jnp.mean(values * values, axis=-1, keepdims=True) + NORM_EPS) * gain_vec
    )


def layout(bounds, token_pos):
    segment = jnp.sum((token_pos[:, None] >= bounds[None, :]).astype(jnp.int32), axis=1)
    starts_all = jnp.concatenate([jnp.zeros((1,), jnp.int32), bounds])
    slot_ids = jnp.arange(bounds.shape[0] + 1, dtype=jnp.int32)
    begin = jnp.sum(
        jnp.where(segment[:, None] == slot_ids[None, :], starts_all[None, :], 0), axis=1
    )
    return (segment, begin)


def exchange_kernel(n_seq, n_fsdp, to_all, x_ref, *refs):
    o_ref, send_sem, recv_sem, own_sem = refs[-4:]
    seq_at, fsdp_at = lax.axis_index("seq"), lax.axis_index("fsdp")
    count = n_seq * n_fsdp
    me = seq_at * n_fsdp + fsdp_at

    def place(step):
        other = lax.rem(me + step, count)
        return other, (other // n_fsdp, lax.rem(other, n_fsdp))

    barrier = pltpu.get_barrier_semaphore()

    def greet(step, carry):
        pl.semaphore_signal(barrier, inc=1, device_id=place(step)[1], device_id_type=MESH)
        return carry

    lax.fori_loop(1, count, greet, 0)
    pl.semaphore_wait(barrier, count - 1)
    own = pltpu.make_async_copy(x_ref if to_all else x_ref.at[me], o_ref.at[me], own_sem)
    own.start()

    def copy(step):
        other, where = place(step)
        return pltpu.make_async_remote_copy(
            src_ref=x_ref if to_all else x_ref.at[other],
            dst_ref=o_ref.at[me],
            send_sem=send_sem.at[step],
            recv_sem=recv_sem.at[step],
            device_id=where,
            device_id_type=MESH,
        )

    def begin(step, carry):
        copy(step).start()
        return carry

    def finish(step, carry):
        copy(step).wait()
        return carry

    lax.fori_loop(1, count, begin, 0)
    own.wait()
    lax.fori_loop(1, count, finish, 0)


def exchange(blocks, to_all, collective_id, after=()):
    n_seq, n_fsdp = lax.axis_size("seq"), lax.axis_size("fsdp")
    count = n_seq * n_fsdp
    shape = (count,) + blocks.shape if to_all else blocks.shape
    return pl.pallas_call(
        functools.partial(exchange_kernel, n_seq, n_fsdp, to_all),
        out_shape=jax.ShapeDtypeStruct(shape, blocks.dtype),
        in_specs=[pl.BlockSpec(memory_space=pl.ANY)] * (1 + len(after)),
        out_specs=pl.BlockSpec(memory_space=pl.ANY),
        scratch_shapes=[
            pltpu.SemaphoreType.DMA((count,)),
            pltpu.SemaphoreType.DMA((count,)),
            pltpu.SemaphoreType.DMA,
        ],
        compiler_params=pltpu.CompilerParams(collective_id=collective_id, has_side_effects=True),
    )(blocks, *after)


def sum_small(values, collective_id):
    rows = -(-values.shape[0] // 1024) * 8
    block = jnp.zeros((rows * 128,), jnp.float32).at[: values.shape[0]].set(values)
    parts = exchange(block.reshape(rows, 128), True, collective_id)
    return jnp.sum(parts, axis=0).reshape(-1)[: values.shape[0]]


def capacity(tokens, owners):
    return -(-(5 * tokens) // (4 * owners * 16)) * 16


def rank_ids(ids, height):
    at = jnp.arange(ids.shape[0], dtype=jnp.int32)
    again = jnp.any((ids[:, None] == ids[None, :]) & (at[None, :] < at[:, None]), axis=1)
    owner = ids // height
    floor = owner * height
    below = (
        (ids[None, :] < ids[:, None]) & (ids[None, :] >= floor[:, None]) & jnp.logical_not(again)[None, :]
    )
    return owner, jnp.sum(below.astype(jnp.int32), axis=1)


def slot_lists(ids, owner, rank, start, size, owners, height):
    within = rank - start
    valid = (within >= 0) & (within < size)
    slot = jnp.where(valid, owner * size + within, -1)
    slot_ids = jnp.arange(owners * size, dtype=jnp.int32)
    rows = jnp.max(
        jnp.where(slot[None, :] == slot_ids[:, None], (ids - owner * height)[None, :], -1), axis=1
    )
    return slot, rows.reshape(owners, size)


def pick_rows(table, wanted):
    count, size = wanted.shape
    rows = jnp.take(table, jnp.maximum(wanted, 0).reshape(-1), axis=0)
    return lax.optimization_barrier(rows).astype(jnp.bfloat16).reshape(count, size, table.shape[1])


def one_hot(slot, slots):
    return (slot[:, None] == jnp.arange(slots, dtype=jnp.int32)[None, :]).astype(jnp.bfloat16)


def spread_rows(arrived, slot, n_seq):
    count, size, columns = arrived.shape
    chosen = one_hot(slot, count // n_seq * size)
    parts = arrived.reshape(n_seq, -1, columns)
    return jnp.concatenate(
        [jnp.dot(chosen, parts[s], preferred_element_type=jnp.float32) for s in range(n_seq)], axis=1
    ).astype(jnp.bfloat16)


def collect_rows(token_grad, slot, n_seq, n_fsdp, size):
    chosen = one_hot(slot, n_fsdp * size)
    columns = token_grad.shape[1] // n_seq
    parts = [
        lax.dot_general(
            chosen,
            token_grad[:, s * columns : (s + 1) * columns],
            (((0,), (0,)), ((), ())),
            preferred_element_type=jnp.float32,
        )
        .astype(jnp.bfloat16)
        .reshape(n_fsdp, size, columns)
        for s in range(n_seq)
    ]
    return jnp.concatenate(parts, axis=0)


def embed_forward(token_ids, table):
    n_seq, n_fsdp = lax.axis_size("seq"), lax.axis_size("fsdp")
    ids = token_ids.reshape(-1)
    tokens, height = ids.shape[0], table.shape[0]
    size = capacity(tokens, n_fsdp)
    owner, rank = rank_ids(ids, height)
    slot, rows = slot_lists(ids, owner, rank, 0, size, n_fsdp, height)
    width = -(-(size + 1) // 1024) * 1024
    note = jnp.zeros((n_fsdp, width), jnp.int32)
    note = note.at[:, :size].set(rows).at[:, size].set(jnp.max(rank))
    note = note.reshape(n_fsdp, width // 128, 128)
    note = jnp.concatenate([note] * n_seq, axis=0)
    heard = exchange(note, False, 1).reshape(n_seq * n_fsdp, width)
    wanted = heard[:, :size]
    most = jnp.max(heard[:, size])
    arrived = exchange(pick_rows(table, wanted), False, 2)

    def plain(arrived):
        return spread_rows(arrived, slot, n_seq)

    def rounds(arrived):
        def another(carry):
            start, total = carry
            slot, rows = slot_lists(ids, owner, rank, start, size, n_fsdp, height)
            wanted = lax.all_to_all(
                jnp.concatenate([rows] * n_seq, axis=0), ("seq", "fsdp"), 0, 0, tiled=True
            )
            own_table = lax.optimization_barrier((table, start))[0]
            arrived = lax.all_to_all(pick_rows(own_table, wanted), ("seq", "fsdp"), 0, 0, tiled=True)
            return start + size, total + spread_rows(arrived, slot, n_seq)

        return lax.while_loop(lambda carry: carry[0] <= most, another, (jnp.int32(size), plain(arrived)))[1]

    embedded = lax.cond(most < size, plain, rounds, arrived)
    return embedded, (ids, owner, rank, slot, wanted, most, size)


def add_rows(total, arrived, wanted):
    height = total.shape[0]
    target = jnp.where(wanted >= 0, wanted, height).reshape(-1)
    rows = arrived.reshape(target.shape[0], -1).astype(jnp.float32)
    return total.at[target].add(rows, mode="drop")


def scatter_kernel(size, wanted_ref, count_ref, arrived_ref, *refs):
    total_ref, square_ref, rows_ref = refs[-3:]
    sources = arrived_ref.shape[0]
    height = total_ref.shape[0]

    def clear(i, carry):
        at = pl.ds(pl.multiple_of(i * 8, 8), 8)
        total_ref[at, :] = jnp.zeros((8, total_ref.shape[1]), jnp.float32)
        return carry

    whole = height // 8
    lax.fori_loop(0, whole, clear, 0, unroll=8)
    if height % 8:
        total_ref[whole * 8 :, :] = jnp.zeros((height % 8, total_ref.shape[1]), jnp.float32)

    def one_source(k, carry):
        rows_ref[...] = arrived_ref[k].astype(jnp.float32)
        count = count_ref[k]

        def four(i, inner):
            first = i * 4
            at = [wanted_ref[k * size + first + n] for n in range(4)]
            sums = [total_ref[pl.ds(at[n], 1), :] + rows_ref[pl.ds(first + n, 1), :] for n in range(4)]
            for n in range(4):
                total_ref[pl.ds(at[n], 1), :] = sums[n]
            return inner

        def one(i, inner):
            at = wanted_ref[k * size + i]
            total_ref[pl.ds(at, 1), :] += rows_ref[pl.ds(i, 1), :]
            return inner

        lax.fori_loop(0, count // 4, four, 0)
        lax.fori_loop(count // 4 * 4, count, one, 0)
        return carry

    lax.fori_loop(0, sources, one_source, 0)

    def add_square(i, carry):
        block = total_ref[pl.ds(pl.multiple_of(i * 8, 8), 8), :]
        return carry + block * block

    partial = lax.fori_loop(0, whole, add_square, jnp.zeros((8, total_ref.shape[1]), jnp.float32), unroll=8)
    if height % 8:
        rest = total_ref[whole * 8 :, :]
        partial = partial + jnp.concatenate(
            [rest * rest, jnp.zeros((8 - height % 8, total_ref.shape[1]), jnp.float32)], axis=0
        )
    square_ref[...] = partial


def scatter_rows(arrived, wanted, height, after):
    sources, size, width = arrived.shape
    counts = jnp.sum((wanted >= 0).astype(jnp.int32), axis=1)
    vmem = pl.BlockSpec(memory_space=pltpu.VMEM)
    return pl.pallas_call(
        functools.partial(scatter_kernel, size),
        grid_spec=pltpu.PrefetchScalarGridSpec(
            num_scalar_prefetch=2,
            grid=(),
            in_specs=[vmem] + [pl.BlockSpec(memory_space=pl.ANY)] * len(after),
            out_specs=[vmem, vmem],
            scratch_shapes=[pltpu.VMEM((size, width), jnp.float32)],
        ),
        out_shape=[
            jax.ShapeDtypeStruct((height, width), jnp.float32),
            jax.ShapeDtypeStruct((8, width), jnp.float32),
        ],
        compiler_params=pltpu.CompilerParams(vmem_limit_bytes=VMEM_BYTES),
        cost_estimate=pl.CostEstimate(flops=10**9, bytes_accessed=80 * 2**20, transcendentals=0),
    )(wanted.reshape(-1), counts, arrived, *after)


def embed_send(token_grad, kept, after):
    n_seq, n_fsdp = lax.axis_size("seq"), lax.axis_size("fsdp")
    slot, size = kept[3], kept[6]
    return exchange(collect_rows(token_grad, slot, n_seq, n_fsdp, size), False, 5, after)


def embed_backward(token_grad, arrived, kept, height, after):
    n_seq, n_fsdp = lax.axis_size("seq"), lax.axis_size("fsdp")
    ids, owner, rank, slot, wanted, most, size = kept

    def plain(arrived, *after):
        total, squares = scatter_rows(arrived, wanted, height, after)
        return total, jnp.sum(squares)

    def rounds(arrived, *after):
        def another(carry):
            start, total = carry
            slot, rows = slot_lists(ids, owner, rank, start, size, n_fsdp, height)
            wanted = lax.all_to_all(
                jnp.concatenate([rows] * n_seq, axis=0), ("seq", "fsdp"), 0, 0, tiled=True
            )
            arrived = lax.all_to_all(
                collect_rows(token_grad, slot, n_seq, n_fsdp, size), ("seq", "fsdp"), 0, 0, tiled=True
            )
            return start + size, add_rows(total, arrived, wanted)

        total = plain(arrived, *after)[0]
        total = lax.while_loop(lambda carry: carry[0] <= most, another, (jnp.int32(size), total))[1]
        return total, jnp.sum(total * total)

    return lax.cond(most < size, plain, rounds, arrived, *after)


ANY = pl.BlockSpec(memory_space=pl.ANY)
HALF = KEY_VALUE_HEADS // 2


def turn(values):
    return pltpu.roll(values, HEAD_SIZE // 2, axis=1)


def columns(head):
    return slice(head * HEAD_SIZE, (head + 1) * HEAD_SIZE)


def shape_head(raw, cosine, sine, gain):
    raw = raw.astype(jnp.float32)
    scale = lax.rsqrt(jnp.mean(raw * raw, axis=-1, keepdims=True) + NORM_EPS)
    normed = raw * scale * gain
    return (normed * cosine + turn(normed) * sine).astype(jnp.bfloat16)


def shape_head_back(raw, cosine, sine, gain, grad):
    raw = raw.astype(jnp.float32)
    scale = lax.rsqrt(jnp.mean(raw * raw, axis=-1, keepdims=True) + NORM_EPS)
    grad = grad * cosine + turn(grad * sine)
    unit = raw * scale
    gain_grad = jnp.sum(grad * unit, axis=0, keepdims=True)
    grad = grad * gain
    inner = jnp.mean(grad * unit, axis=-1, keepdims=True)
    return (scale * (grad - unit * inner)).astype(jnp.bfloat16), gain_grad


def queries_kernel(raw_ref, cos_ref, sin_ref, gain_ref, out_ref):
    for head in range(QUERY_HEADS):
        at = columns(head)
        out_ref[:, at] = shape_head(raw_ref[:, at], cos_ref[...], sin_ref[...], gain_ref[0:1, :])


def keys_kernel(raw_ref, cos_ref, sin_ref, gain_ref, *out_refs):
    for head in range(KEY_VALUE_HEADS):
        out_ref = out_refs[head // HALF]
        out_ref[:, columns(head % HALF)] = shape_head(
            raw_ref[:, columns(head)], cos_ref[...], sin_ref[...], gain_ref[1:2, :]
        )
    for half in range(2):
        first = KEY_COLS + half * HALF * HEAD_SIZE
        out_refs[half][:, HALF * HEAD_SIZE :] = raw_ref[:, first : first + HALF * HEAD_SIZE]


def token_blocks(rows, width):
    return pl.BlockSpec((rows, width), lambda i: (i, 0))


def shape_queries(raw, cosine, sine, gains):
    tokens = raw.shape[0]
    rows = min(256, tokens)
    return pl.pallas_call(
        queries_kernel,
        grid=(tokens // rows,),
        in_specs=[
            token_blocks(rows, QUERY_COLS),
            token_blocks(rows, HEAD_SIZE),
            token_blocks(rows, HEAD_SIZE),
            pl.BlockSpec((2, HEAD_SIZE), lambda i: (0, 0)),
        ],
        out_specs=token_blocks(rows, QUERY_COLS),
        out_shape=jax.ShapeDtypeStruct((tokens, QUERY_COLS), jnp.bfloat16),
        compiler_params=pltpu.CompilerParams(vmem_limit_bytes=VMEM_BYTES),
        cost_estimate=pl.CostEstimate(flops=4 * 10**9, bytes_accessed=8 * 2**20, transcendentals=0),
    )(raw, cosine, sine, gains)


def shape_keys(raw, cosine, sine, gains):
    tokens = raw.shape[0]
    rows = min(256, tokens)
    half = jax.ShapeDtypeStruct((tokens, KEY_COLS), jnp.bfloat16)
    return pl.pallas_call(
        keys_kernel,
        grid=(tokens // rows,),
        in_specs=[
            token_blocks(rows, 2 * KEY_COLS),
            token_blocks(rows, HEAD_SIZE),
            token_blocks(rows, HEAD_SIZE),
            pl.BlockSpec((2, HEAD_SIZE), lambda i: (0, 0)),
        ],
        out_specs=[token_blocks(rows, KEY_COLS)] * 2,
        out_shape=[half, half],
        compiler_params=pltpu.CompilerParams(vmem_limit_bytes=VMEM_BYTES),
        cost_estimate=pl.CostEstimate(flops=2 * 10**9, bytes_accessed=8 * 2**20, transcendentals=0),
    )(raw, cosine, sine, gains)


def add_gain_grad(gain_ref, total):
    @pl.when(pl.program_id(0) == 0)
    def _():
        gain_ref[...] = jnp.zeros_like(gain_ref)

    gain_ref[0:1, :] += total


def queries_back_kernel(raw_ref, cos_ref, sin_ref, gain_ref, dq_ref, *refs):
    out_ref, dgain_ref = refs[-2:]
    total = jnp.zeros((1, HEAD_SIZE), jnp.float32)
    for head in range(QUERY_HEADS):
        at = columns(head)
        grad = dq_ref[:, at].astype(jnp.float32)
        out_ref[:, at], part = shape_head_back(raw_ref[:, at], cos_ref[...], sin_ref[...], gain_ref[0:1, :], grad)
        total = total + part
    add_gain_grad(dgain_ref, total)


def keys_back_kernel(raw_ref, cos_ref, sin_ref, gain_ref, own_a_ref, own_b_ref, more_a_ref, more_b_ref, out_ref, dgain_ref):
    total = jnp.zeros((1, HEAD_SIZE), jnp.float32)
    for head in range(KEY_VALUE_HEADS):
        own_ref, more_ref = ((own_a_ref, more_a_ref), (own_b_ref, more_b_ref))[head // HALF]
        at, part_at = columns(head), columns(head % HALF)
        grad = own_ref[0, :, part_at] + more_ref[0, :, part_at].astype(jnp.float32)
        out_ref[:, at], part = shape_head_back(raw_ref[:, at], cos_ref[...], sin_ref[...], gain_ref[1:2, :], grad)
        total = total + part
    for half, (own_ref, more_ref) in enumerate(((own_a_ref, more_a_ref), (own_b_ref, more_b_ref))):
        first = KEY_COLS + half * HALF * HEAD_SIZE
        out_ref[:, first : first + HALF * HEAD_SIZE] = (
            own_ref[1] + more_ref[1].astype(jnp.float32)
        ).astype(jnp.bfloat16)
    add_gain_grad(dgain_ref, total)


def shape_back(kernel, raw, cosine, sine, gains, grads, after=()):
    tokens = raw.shape[0]
    rows = min(128, tokens)
    wide = [
        pl.BlockSpec((2, rows, g.shape[2]), lambda i: (0, i, 0)) if g.ndim == 3 else token_blocks(rows, g.shape[1])
        for g in grads
    ]
    return pl.pallas_call(
        kernel,
        grid=(tokens // rows,),
        in_specs=[
            token_blocks(rows, raw.shape[1]),
            token_blocks(rows, HEAD_SIZE),
            token_blocks(rows, HEAD_SIZE),
            pl.BlockSpec((2, HEAD_SIZE), lambda i: (0, 0)),
        ]
        + wide
        + [ANY] * len(after),
        out_specs=[token_blocks(rows, raw.shape[1]), pl.BlockSpec((8, HEAD_SIZE), lambda i: (0, 0))],
        out_shape=[
            jax.ShapeDtypeStruct(raw.shape, jnp.bfloat16),
            jax.ShapeDtypeStruct((8, HEAD_SIZE), jnp.float32),
        ],
        compiler_params=pltpu.CompilerParams(vmem_limit_bytes=VMEM_BYTES),
        cost_estimate=pl.CostEstimate(flops=5 * 10**9, bytes_accessed=20 * 2**20, transcendentals=0),
    )(raw, cosine, sine, gains, *grads, *after)


def both_heads(block):
    return jnp.concatenate([block[:, :HEAD_SIZE], block[:, HEAD_SIZE:]], axis=0)


def key_ranges(scalar_ref, step, rows, keys):
    first_own, first_before, low = scalar_ref[0], scalar_ref[1], scalar_ref[2 + 2 * step]
    before = (jnp.minimum(low, first_own) - first_before) // keys, (first_own - first_before) // keys
    own = jnp.maximum(low - first_own, 0) // keys, ((step + 1) * rows - 1) // keys + 1
    return first_own, first_before, before, own


def allowed_keys(begin_ref, offset, rows, keys):
    begin = begin_ref[...] - offset
    at = lax.broadcasted_iota(jnp.int32, (rows, 1), 0)
    key_at = lax.broadcasted_iota(jnp.int32, (rows, keys), 1)
    return begin, at, key_at


def visit_blocks(scalar_ref, begin_ref, rows, keys, refs, work):
    step = pl.program_id(1)
    first_own, first_before, before, own = key_ranges(scalar_ref, step, rows, keys)
    first_row = first_own + step * rows
    last_begin = scalar_ref[3 + 2 * step]

    def run(bounds, base, group):
        def one(j, carry):
            at = pl.ds(pl.multiple_of(j * keys, keys), keys)
            first_key = base + j * keys
            whole = (first_key + keys - 1 <= first_row) & (first_key >= last_begin)

            @pl.when(whole)
            def _():
                work(*group, at, None)

            @pl.when(jnp.logical_not(whole))
            def _():
                begin = begin_ref[...] - first_key
                row = (first_row - first_key) + lax.broadcasted_iota(jnp.int32, (rows, 1), 0)
                key = lax.broadcasted_iota(jnp.int32, (rows, keys), 1)
                work(*group, at, (key <= row) & (key >= begin))

            return carry

        lax.fori_loop(bounds[0], bounds[1], one, 0)

    run(before, first_before, refs[0])
    run(own, first_own, refs[1])


def forward_kernel(keys, scalar_ref, q_ref, kb_ref, vb_ref, k_ref, v_ref, begin_ref, *refs):
    o_ref, lse_ref, acc_ref = refs[-3:]
    rows = q_ref.shape[0]
    query = both_heads(q_ref[...])
    acc_ref[...] = jnp.zeros_like(acc_ref)
    ones = jnp.ones((keys, HEAD_SIZE), jnp.bfloat16)

    def work(key_ref, value_ref, at, mask):
        value = jnp.concatenate([value_ref[at, :], ones], axis=1)
        scores = [
            lax.dot_general(
                query[h * rows : (h + 1) * rows], key_ref[at, :], (((1,), (1,)), ((), ())),
                preferred_element_type=jnp.float32,
            )
            for h in range(2)
        ]
        for h in range(2):
            weight = jnp.exp2(scores[h] * (LOG2E * HEAD_SIZE**-0.5))
            if mask is not None:
                weight = jnp.where(mask, weight, 0.0)
            acc_ref[h * rows : (h + 1) * rows, :] += jnp.dot(
                weight.astype(jnp.bfloat16), value, preferred_element_type=jnp.float32
            )

    visit_blocks(scalar_ref, begin_ref, rows, keys, ((kb_ref, vb_ref), (k_ref, v_ref)), work)
    acc = acc_ref[...]
    total = acc[:, HEAD_SIZE : HEAD_SIZE + 1]
    out = (acc[:, :HEAD_SIZE] / total).astype(jnp.bfloat16)
    o_ref[:, :HEAD_SIZE] = out[:rows]
    o_ref[:, HEAD_SIZE:] = out[rows:]
    lse = jnp.log2(total)
    lse_ref[0, :, 0:1] = lse[:rows]
    lse_ref[0, :, 1:2] = lse[rows:]


def attention_specs(tokens, length, rows, first):
    key = lambda h, i, s: (0, h)
    value = lambda h, i, s: (0, HALF + h)
    return [
        pl.BlockSpec((rows, 2 * HEAD_SIZE), lambda h, i, s: (i, first + h)),
        pl.BlockSpec((length, HEAD_SIZE), key),
        pl.BlockSpec((length, HEAD_SIZE), value),
        pl.BlockSpec((tokens, HEAD_SIZE), key),
        pl.BlockSpec((tokens, HEAD_SIZE), value),
        pl.BlockSpec((rows, 1), lambda h, i, s: (i, 0)),
    ]


def attention_forward(scalars, query, before, own, begin, rows, keys, first, filled):
    tokens = query.shape[0]
    specs = attention_specs(tokens, before.shape[0], rows, first)
    return pl.pallas_call(
        functools.partial(forward_kernel, keys),
        grid_spec=pltpu.PrefetchScalarGridSpec(
            num_scalar_prefetch=1,
            grid=(HALF, tokens // rows),
            in_specs=specs + [ANY] * len(filled),
            out_specs=[specs[0], pl.BlockSpec((1, rows, 2), lambda h, i, s: (first + h, i, 0))],
            scratch_shapes=[pltpu.VMEM((2 * rows, 2 * HEAD_SIZE), jnp.float32)],
        ),
        out_shape=[
            jax.ShapeDtypeStruct((tokens, QUERY_COLS), jnp.bfloat16),
            jax.ShapeDtypeStruct((KEY_VALUE_HEADS, tokens, 2), jnp.float32),
        ],
        input_output_aliases={7 + i: i for i in range(len(filled))},
        compiler_params=pltpu.CompilerParams(vmem_limit_bytes=VMEM_BYTES),
        cost_estimate=pl.CostEstimate(flops=20 * 10**9, bytes_accessed=16 * 2**20, transcendentals=10**7),
    )(scalars, query, before, before, own, own, begin, *filled)


def backward_kernel(keys, scalar_ref, q_ref, kb_ref, vb_ref, k_ref, v_ref, begin_ref, do_ref, o_ref, lse_ref, *refs):
    dq_ref, before_ref, own_ref, acc_ref, dq_acc_ref = refs[-5:]
    step = pl.program_id(1)
    rows = q_ref.shape[0]
    query = both_heads(q_ref[...])
    grad = both_heads(do_ref[...])
    out = both_heads(o_ref[...])
    lse = jnp.concatenate([lse_ref[0, :, 0:1], lse_ref[0, :, 1:2]], axis=0)
    inner = jnp.sum(grad.astype(jnp.float32) * out.astype(jnp.float32), axis=-1, keepdims=True)

    @pl.when(step == 0)
    def _():
        acc_ref[...] = jnp.zeros_like(acc_ref)
        own_ref[...] = jnp.zeros_like(own_ref)

    dq_acc_ref[...] = jnp.zeros_like(dq_acc_ref)

    def work(key_ref, value_ref, sum_ref, at, mask):
        key = key_ref[at, :]
        score = lax.dot_general(query, key, (((1,), (1,)), ((), ())), preferred_element_type=jnp.float32)
        prob_grad = lax.dot_general(
            grad, value_ref[at, :], (((1,), (1,)), ((), ())), preferred_element_type=jnp.float32
        )
        prob = jnp.exp2(score * (LOG2E * HEAD_SIZE**-0.5) - lse)
        if mask is not None:
            prob = jnp.where(jnp.concatenate([mask, mask], axis=0), prob, 0.0)
        sum_ref[1, at, :] += lax.dot_general(
            prob.astype(jnp.bfloat16), grad, (((0,), (0,)), ((), ())), preferred_element_type=jnp.float32
        )
        score_grad = (prob * (prob_grad - inner)).astype(jnp.bfloat16)
        sum_ref[0, at, :] += lax.dot_general(
            score_grad, query, (((0,), (0,)), ((), ())), preferred_element_type=jnp.float32
        )
        dq_acc_ref[...] += jnp.dot(score_grad, key, preferred_element_type=jnp.float32)

    visit_blocks(
        scalar_ref, begin_ref, rows, keys, ((kb_ref, vb_ref, acc_ref), (k_ref, v_ref, own_ref)), work
    )
    dq = dq_acc_ref[...] * HEAD_SIZE**-0.5
    dq_ref[:, :HEAD_SIZE] = dq[:rows]
    dq_ref[:, HEAD_SIZE:] = dq[rows:]

    @pl.when(step == pl.num_programs(1) - 1)
    def _():
        own_ref[0] = own_ref[0] * HEAD_SIZE**-0.5
        before_ref[0] = (acc_ref[0] * HEAD_SIZE**-0.5).astype(before_ref.dtype)
        before_ref[1] = acc_ref[1].astype(before_ref.dtype)


def attention_backward(scalars, query, before, own, begin, grad_out, out, lse, rows, keys, first, filled, after):
    tokens, length = query.shape[0], before.shape[0]
    specs = attention_specs(tokens, length, rows, first)
    both = lambda h, i, s: (0, 0, h)
    before_type = jnp.bfloat16 if length == tokens else jnp.float32
    return pl.pallas_call(
        functools.partial(backward_kernel, keys),
        grid_spec=pltpu.PrefetchScalarGridSpec(
            num_scalar_prefetch=1,
            grid=(HALF, tokens // rows),
            in_specs=specs
            + [specs[0], specs[0], pl.BlockSpec((1, rows, 2), lambda h, i, s: (first + h, i, 0))]
            + [ANY] * (len(filled) + len(after)),
            out_specs=[
                specs[0],
                pl.BlockSpec((2, length, HEAD_SIZE), both),
                pl.BlockSpec((2, tokens, HEAD_SIZE), both),
            ],
            scratch_shapes=[
                pltpu.VMEM((2, length, HEAD_SIZE), jnp.float32),
                pltpu.VMEM((2 * rows, HEAD_SIZE), jnp.float32),
            ],
        ),
        out_shape=[
            jax.ShapeDtypeStruct((tokens, QUERY_COLS), jnp.float32),
            jax.ShapeDtypeStruct((2, length, HALF * HEAD_SIZE), before_type),
            jax.ShapeDtypeStruct((2, tokens, HALF * HEAD_SIZE), jnp.float32),
        ],
        input_output_aliases={10 + i: i for i in range(len(filled))},
        compiler_params=pltpu.CompilerParams(vmem_limit_bytes=VMEM_BYTES),
        cost_estimate=pl.CostEstimate(flops=40 * 10**9, bytes_accessed=40 * 2**20, transcendentals=10**7),
    )(scalars, query, before, before, own, own, begin, grad_out, out, lse, *filled, *after)


def tokens_before(own):
    if lax.axis_size("seq") != 2:
        return lax.all_gather(own, "seq", axis=0, tiled=True)
    return lax.ppermute(own, "seq", [(0, 1), (1, 0)])


def to_tokens_before(parts):
    if lax.axis_size("seq") != 2:
        return lax.psum_scatter(parts, "seq", scatter_dimension=1, tiled=True)
    return lax.ppermute(parts, "seq", [(0, 1), (1, 0)])


def fetch(weight):
    return lax.all_gather(weight.astype(jnp.bfloat16), ("seq", "fsdp"), axis=0, tiled=True)


def trade(values, axis, bit):
    count = lax.axis_size(axis)
    return lax.ppermute(values, axis, [(i, i ^ bit) for i in range(count)])


def halves(values, dim, at):
    return (
        lax.dynamic_index_in_dim(values, at, dim, keepdims=False),
        lax.dynamic_index_in_dim(values, 1 - at, dim, keepdims=False),
    )


def by_stages():
    return (lax.axis_size("seq"), lax.axis_size("fsdp")) == (2, 16)


def where_am_i():
    at = lax.axis_index("fsdp")
    return lax.axis_index("seq"), at >> 2, (at >> 1) & 1, at & 1


def gradient_kernel(height, core_ref, left_ref, right_ref, *refs):
    keep_ref, send_ref, turned_ref = refs[-3:]

    @pl.when(pl.program_id(1) == 0)
    def _():
        turned_ref[...] = left_ref[...].T

    product = jnp.dot(turned_ref[...], right_ref[...], preferred_element_type=jnp.float32)
    even = core_ref[0] == 0
    for p in range(keep_ref.shape[0]):
        first = product[2 * p * height : (2 * p + 1) * height]
        second = product[(2 * p + 1) * height : (2 * p + 2) * height]
        keep_ref[p] = jnp.where(even, first, second).astype(jnp.bfloat16)
        send_ref[p] = jnp.where(even, second, first).astype(jnp.bfloat16)


def gradient_blocks(left, right, rows, place, packed_rows, filled):
    tokens, tall = left.shape
    height = tall // 32
    pairs = rows // (2 * height)
    out = jax.ShapeDtypeStruct((16, packed_rows, D), jnp.bfloat16)
    block = pl.BlockSpec((pairs, height, D), lambda i, j, s: (i, place(j), 0))
    return pl.pallas_call(
        functools.partial(gradient_kernel, height),
        grid_spec=pltpu.PrefetchScalarGridSpec(
            num_scalar_prefetch=1,
            grid=(tall // rows, right.shape[1] // D),
            in_specs=[
                pl.BlockSpec((tokens, rows), lambda i, j, s: (0, i)),
                pl.BlockSpec((tokens, D), lambda i, j, s: (0, j)),
            ]
            + [ANY] * len(filled),
            out_specs=[block, block],
            scratch_shapes=[pltpu.VMEM((rows, tokens), jnp.bfloat16)],
        ),
        out_shape=[out, out],
        input_output_aliases={3 + i: i for i in range(len(filled))},
        compiler_params=pltpu.CompilerParams(vmem_limit_bytes=VMEM_BYTES),
        cost_estimate=pl.CostEstimate(
            flops=2 * tokens * tall * right.shape[1], bytes_accessed=16 * 2**20, transcendentals=0
        ),
    )(where_am_i()[3].reshape(1), left, right, *filled)


def core_kernel(at_ref, keep_ref, got_ref, left_keep_ref, left_send_ref, right_keep_ref, right_send_ref):
    y_other, x_other = pl.program_id(0), pl.program_id(1)
    total = (keep_ref[0].astype(jnp.float32) + got_ref[0].astype(jnp.float32)).astype(jnp.bfloat16)
    left, right = total[:, : D // 2], total[:, D // 2 :]

    @pl.when(y_other == 0)
    def _():
        left_keep_ref[0, 0] = left

    @pl.when(y_other == 1)
    def _():
        left_send_ref[0, 0] = left

    @pl.when(x_other == 0)
    def _():
        right_keep_ref[0, 0] = right

    @pl.when(x_other == 1)
    def _():
        right_send_ref[0, 0] = right


def sum_core(keep, send):
    rows = keep.shape[1]
    got = trade(send, "fsdp", 1)
    y_at, _, x_at, _ = where_am_i()

    def chip(a, b, z, s):
        return (((a ^ s[0]) * 4 + z) * 2 + (b ^ s[1]), 0, 0)

    def left_keep(a, b, z, s):
        return (jnp.where(a == 0, z, 3), jnp.where(a == 0, b, 1) ^ s[1], 0, 0)

    def left_send(a, b, z, s):
        return (jnp.where(a == 1, z, 0), jnp.where(a == 1, b, 0) ^ s[1], 0, 0)

    def right_keep(a, b, z, s):
        return (a ^ s[0], jnp.where(b == 0, z, 3), 0, 0)

    def right_send(a, b, z, s):
        return (jnp.where(b == 1, a, 0) ^ s[0], jnp.where(b == 1, z, jnp.where(a == 0, 0, 3)), 0, 0)

    full = pl.BlockSpec((1, rows, D), chip)
    part = lambda index: pl.BlockSpec((1, 1, rows, D // 2), index)
    left = jax.ShapeDtypeStruct((4, 2, rows, D // 2), jnp.bfloat16)
    right = jax.ShapeDtypeStruct((2, 4, rows, D // 2), jnp.bfloat16)
    lk, ls, rk, rs = pl.pallas_call(
        core_kernel,
        grid_spec=pltpu.PrefetchScalarGridSpec(
            num_scalar_prefetch=1,
            grid=(2, 2, 4),
            in_specs=[full, full],
            out_specs=[part(left_keep), part(left_send), part(right_keep), part(right_send)],
        ),
        out_shape=[left, left, right, right],
        compiler_params=pltpu.CompilerParams(vmem_limit_bytes=VMEM_BYTES),
        cost_estimate=pl.CostEstimate(flops=10**9, bytes_accessed=96 * 2**10 * rows, transcendentals=0),
    )(jnp.stack([y_at, x_at]), keep, got)
    return (lk, rk), (ls, rs)


def sum_first(keep, send, after=0.0):
    y_at, _, x_at, _ = where_am_i()
    low, wide = jnp.bfloat16, jnp.float32
    left = keep[0].astype(wide) + trade(send[0], "seq", 1).astype(wide) + after
    right = keep[1].astype(wide) + trade(send[1], "fsdp", 2).astype(wide) + after
    left_keep, left_send = halves(left, 1, x_at)
    right_keep, right_send = halves(right, 0, y_at)
    return (left_keep, right_keep), (left_send.astype(low), right_send.astype(low))


def sum_second(keep, send, after=0.0):
    z_at = where_am_i()[1]
    left = keep[0] + trade(send[0], "fsdp", 2).astype(jnp.float32) + after
    right = keep[1] + trade(send[1], "seq", 1).astype(jnp.float32) + after
    total = jnp.concatenate([left, right], axis=-1)
    own = lax.dynamic_index_in_dim(total, z_at, 0, keepdims=False)
    sends = tuple(
        lax.dynamic_index_in_dim(total, z_at ^ other, 0, keepdims=False).astype(jnp.bfloat16) for other in (1, 2, 3)
    )
    return own, sends


def sum_last(keep, send):
    total = keep
    for other in (1, 2, 3):
        total = total + trade(send[other - 1], "fsdp", 4 * other).astype(jnp.float32)
    return total


def beside(total, height, starts):
    return jnp.concatenate([total[r : r + height] for r in starts], axis=1)


def plain_sum(left, right):
    grad = lax.dot_general(left, right, (((0,), (0,)), ((), ())), preferred_element_type=jnp.float32)
    return lax.psum_scatter(grad, ("seq", "fsdp"), scatter_dimension=0, tiled=True)


def adam_update(weight, moment_one, moment_two, grad, factor, step_float):
    grad = grad * factor
    moment_one = BETA_ONE * moment_one + (1.0 - BETA_ONE) * grad
    moment_two = BETA_TWO * moment_two + (1.0 - BETA_TWO) * grad * grad
    fix_one = 1.0 - BETA_ONE**step_float
    fix_two = 1.0 - BETA_TWO**step_float
    weight = weight - LEARN_RATE * (
        moment_one / fix_one / (jnp.sqrt(moment_two / fix_two) + ADAM_EPS) + WEIGHT_DECAY * weight
    )
    return (weight, moment_one, moment_two)


def body(
    token_ids,
    seq_lengths,
    pairing,
    step_count,
    embedding,
    embedding_one,
    embedding_two,
    qkv_weight,
    qkv_one,
    qkv_two,
    out_weight,
    out_one,
    out_two,
    gate_up_weight,
    gate_up_one,
    gate_up_two,
    down_weight,
    down_one,
    down_two,
    norm_gains,
    gains_one,
    gains_two,
    score_weight,
    score_one,
    score_two,
):
    seq_at = lax.axis_index("seq")
    group_at = lax.axis_index("fsdp")
    token_rows = token_ids.shape[1]
    per_group = seq_lengths.shape[1] - 1
    lengths = seq_lengths[0]
    bounds = jnp.stack([jnp.sum(lengths[: j + 1]) for j in range(per_group)])
    token_pos = seq_at * token_rows + jnp.arange(token_rows, dtype=jnp.int32)
    segment, begin = layout(bounds, token_pos)
    frequency = ROPE_THETA ** (
        -2.0 * jnp.arange(HEAD_SIZE // 2, dtype=jnp.float32) / HEAD_SIZE
    )
    angles = (token_pos - begin).astype(jnp.float32)[:, None] * frequency[None, :]
    cosine, sine = jnp.cos(angles), jnp.sin(angles)
    cosine = jnp.concatenate([cosine, cosine], axis=1)
    sine = jnp.concatenate([-sine, sine], axis=1)
    query_rows = min(512, token_rows)
    key_rows = min(512, token_rows)
    begin_column = begin[:, None]
    attn_gain = norm_gains[:D]
    mlp_gain = norm_gains[D : 2 * D]
    final_gain = norm_gains[2 * D : 3 * D]
    head_gains = norm_gains[3 * D :].reshape(2, HEAD_SIZE)
    first_own = seq_at * token_rows
    first_before = first_own - token_rows if lax.axis_size("seq") == 2 else 0 * first_own
    scalars = jnp.concatenate(
        [
            jnp.stack([first_own, first_before]),
            jnp.stack([begin[::query_rows], begin[query_rows - 1 :: query_rows]], axis=1).reshape(-1),
        ]
    )
    qkv_full = fetch(qkv_weight)
    out_full, gate_up_full, down_full = fetch(out_weight), fetch(gate_up_weight), fetch(down_weight)
    embedded, kept = embed_forward(token_ids, embedding)
    resid_in = embedded.astype(jnp.float32)
    normed_low = rms_norm(resid_in, attn_gain).astype(jnp.bfloat16)
    key_value_raw = jnp.dot(
        normed_low, qkv_full[:, QUERY_COLS:], preferred_element_type=jnp.float32
    ).astype(jnp.bfloat16)
    own_a, own_b = shape_keys(key_value_raw, cosine, sine, head_gains)
    before_a, before_b = tokens_before(own_a), tokens_before(own_b)
    query_raw = jnp.dot(
        normed_low, qkv_full[:, :QUERY_COLS], preferred_element_type=jnp.float32
    ).astype(jnp.bfloat16)
    query_low = shape_queries(query_raw, cosine, sine, head_gains)
    results = attention_forward(
        scalars, query_low, before_a, own_a, begin_column, query_rows, key_rows, 0, ()
    )
    merged, lse = attention_forward(
        scalars, query_low, before_b, own_b, begin_column, query_rows, key_rows, HALF, tuple(results)
    )
    resid_mid = resid_in + jnp.dot(merged, out_full, preferred_element_type=jnp.float32)
    normed_two = rms_norm(resid_mid, mlp_gain).astype(jnp.bfloat16)
    gate_up = jnp.dot(normed_two, gate_up_full, preferred_element_type=jnp.float32)
    activated = (jax.nn.silu(gate_up[:, :FF]) * gate_up[:, FF:]).astype(jnp.bfloat16)
    resid_out = resid_mid + jnp.dot(activated, down_full, preferred_element_type=jnp.float32)
    final = rms_norm(resid_out, final_gain)
    per_token = jnp.sum(final * score_weight, axis=1)
    slot_list = jnp.arange(per_group, dtype=jnp.int32)
    seq_size = seq_lengths[0, :per_group].astype(jnp.float32)
    picker = (segment[None, :] == slot_list[:, None]).astype(jnp.float32) / seq_size[:, None]
    own_scores = jnp.sum(picker * per_token[None, :], axis=1)
    seq_total = pairing.shape[0]
    score_board = lax.dynamic_update_slice(
        jnp.zeros((seq_total,), jnp.float32), own_scores, (group_at * per_group,)
    )
    all_scores = sum_small(score_board, 3)
    pair_table = pairing.reshape(-1, 2)
    seq_ids = jnp.arange(seq_total, dtype=jnp.int32)
    choose = (pair_table[:, 0:1] == seq_ids[None, :]).astype(jnp.float32)
    reject = (pair_table[:, 1:2] == seq_ids[None, :]).astype(jnp.float32)
    margin = jnp.sum((choose - reject) * all_scores[None, :], axis=1)
    ranking_loss = jnp.sum(jax.nn.softplus(-margin))
    margin_grad = -jax.nn.sigmoid(-margin)
    score_grads = jnp.sum(margin_grad[:, None] * (choose - reject), axis=0)
    own_grads = lax.dynamic_slice_in_dim(score_grads, group_at * per_group, per_group)
    token_grad = jnp.sum(own_grads[:, None] * picker, axis=0)
    score_part = jnp.sum(token_grad[:, None] * final, axis=0)
    final_grad = token_grad[:, None] * score_weight[None, :]
    final_back = jax.vjp(rms_norm, resid_out, final_gain)[1]
    dresid_out, dfinal_gain = final_back(final_grad)
    mlp_low = dresid_out.astype(jnp.bfloat16)
    staged = by_stages()
    if staged:
        early = gradient_blocks(activated, mlp_low, 768, lambda j: 0, 352, ())
    else:
        down_shard = plain_sum(activated, mlp_low)
    act_grad = jnp.dot(mlp_low, down_full.T, preferred_element_type=jnp.float32)
    act_back = jax.vjp(lambda joined: jax.nn.silu(joined[:, :FF]) * joined[:, FF:], gate_up)[1]
    gate_up_low = act_back(act_grad)[0].astype(jnp.bfloat16)
    if staged:
        early = gradient_blocks(
            normed_two, gate_up_low, 512, lambda j: jnp.where(j < 3, 3 + j, 5 + j), 352, tuple(early)
        )
    else:
        gate_up_shard = plain_sum(normed_two, gate_up_low)
    normed_two_grad = jnp.dot(gate_up_low, gate_up_full.T, preferred_element_type=jnp.float32)
    mid_back = jax.vjp(rms_norm, resid_mid, mlp_gain)[1]
    mid_extra, dmlp_gain = mid_back(normed_two_grad)
    dresid_mid = dresid_out + mid_extra
    attn_low = dresid_mid.astype(jnp.bfloat16)
    keep, send = (), ()
    if staged:
        early = gradient_blocks(merged, attn_low, 512, lambda j: 3, 352, tuple(early))
        keep, send = sum_core(*early)
    else:
        out_shard = plain_sum(merged, attn_low)
    merged_grad = jnp.dot(attn_low, out_full.T, preferred_element_type=jnp.float32).astype(
        jnp.bfloat16
    )
    common = (begin_column, merged_grad, merged, lse, query_rows, key_rows)
    query_grad, before_grad_a, own_grad_a = attention_backward(
        scalars, query_low, before_a, own_a, *common, 0, (), send
    )
    more_a = to_tokens_before(before_grad_a)
    if staged:
        keep, send = sum_first(keep, send)
    query_grad, before_grad_b, own_grad_b = attention_backward(
        scalars, query_low, before_b, own_b, *common, HALF, (query_grad,), send
    )
    more_b = to_tokens_before(before_grad_b)
    if staged:
        keep, send = sum_second(keep, send)
    query_raw_grad, query_sums = shape_back(
        queries_back_kernel, query_raw, cosine, sine, head_gains, (query_grad,), send
    )
    key_value_raw_grad, key_sums = shape_back(
        keys_back_kernel, key_value_raw, cosine, sine, head_gains, (own_grad_a, own_grad_b, more_a, more_b)
    )
    if staged:
        total = sum_last(keep, send)
        down_shard, out_shard = total[:96], total[192:256]
        gate_up_shard = beside(total, 32, (96, 128, 160, 256, 288, 320))
        late = gradient_blocks(normed_low, query_raw_grad, 512, lambda j: j, 128, ())
        late = gradient_blocks(normed_low, key_value_raw_grad, 512, lambda j: 2 + j, 128, tuple(late))
        keep, send = sum_core(*late)
    else:
        send = ()
        qkv_shard = jnp.concatenate(
            [plain_sum(normed_low, query_raw_grad), plain_sum(normed_low, key_value_raw_grad)], axis=1
        )
    normed_grad = jnp.dot(
        query_raw_grad, qkv_full[:, :QUERY_COLS].T, preferred_element_type=jnp.float32
    ) + jnp.dot(key_value_raw_grad, qkv_full[:, QUERY_COLS:].T, preferred_element_type=jnp.float32)
    in_back = jax.vjp(rms_norm, resid_in, attn_gain)[1]
    in_extra, dattn_gain = in_back(normed_grad)
    dresid_in = dresid_mid + in_extra
    token_grad_low = dresid_in.astype(jnp.bfloat16)
    arrived = embed_send(token_grad_low, kept, send)
    if staged:
        keep, send = sum_first(keep, send, arrived[0, 0, 0].astype(jnp.float32) * 0.0)
    embed_grad, square = embed_backward(token_grad_low, arrived, kept, embedding.shape[0], send)
    if staged:
        keep, send = sum_second(keep, send, square * 0.0)
        qkv_shard = beside(sum_last(keep, send), 32, (0, 32, 64, 96))
    shards = (qkv_shard, out_shard, gate_up_shard, down_shard)
    for shard in shards:
        square = square + jnp.sum(shard * shard)
    gain_part = jnp.concatenate([dattn_gain, dmlp_gain, dfinal_gain, query_sums[0], key_sums[0]])
    gain_count = gain_part.shape[0]
    sums = sum_small(jnp.concatenate([gain_part, score_part, square.reshape(1)]), 4)
    gain_sum, score_sum, square_sum = sums[:gain_count], sums[gain_count:-1], sums[-1]
    grad_norm = jnp.sqrt(square_sum + jnp.sum(gain_sum * gain_sum) + jnp.sum(score_sum * score_sum))
    factor = CLIP_NORM / jnp.maximum(grad_norm, CLIP_NORM)
    step_float = step_count[0]
    e_new = adam_update(embedding, embedding_one, embedding_two, embed_grad, factor, step_float)
    q_new = adam_update(qkv_weight, qkv_one, qkv_two, shards[0], factor, step_float)
    o_new = adam_update(out_weight, out_one, out_two, shards[1], factor, step_float)
    g_new = adam_update(gate_up_weight, gate_up_one, gate_up_two, shards[2], factor, step_float)
    d_new = adam_update(down_weight, down_one, down_two, shards[3], factor, step_float)
    n_new = adam_update(norm_gains, gains_one, gains_two, gain_sum, factor, step_float)
    s_new = adam_update(score_weight, score_one, score_two, score_sum, factor, step_float)
    clipped_gains = gain_sum * factor
    return (
        ranking_loss,
        grad_norm,
        e_new[0],
        e_new[1],
        e_new[2],
        q_new[0],
        q_new[1],
        q_new[2],
        o_new[0],
        o_new[1],
        o_new[2],
        g_new[0],
        g_new[1],
        g_new[2],
        d_new[0],
        d_new[1],
        d_new[2],
        clipped_gains,
        n_new[1],
        n_new[2],
        s_new[0],
        s_new[1],
        s_new[2],
    )


def solution(mesh):
    return jax.shard_map(
        body,
        mesh=mesh,
        in_specs=(
            P("fsdp", "seq"),
            P("fsdp", None),
            P(),
            P(),
            P("fsdp", "seq"),
            P("fsdp", "seq"),
            P("fsdp", "seq"),
            P(("seq", "fsdp"), None),
            P(("seq", "fsdp"), None),
            P(("seq", "fsdp"), None),
            P(("seq", "fsdp"), None),
            P(("seq", "fsdp"), None),
            P(("seq", "fsdp"), None),
            P(("seq", "fsdp"), None),
            P(("seq", "fsdp"), None),
            P(("seq", "fsdp"), None),
            P(("seq", "fsdp"), None),
            P(("seq", "fsdp"), None),
            P(("seq", "fsdp"), None),
            P(),
            P(),
            P(),
            P(),
            P(),
            P(),
        ),
        out_specs=(
            P(),
            P(),
            P("fsdp", "seq"),
            P("fsdp", "seq"),
            P("fsdp", "seq"),
            P(("seq", "fsdp"), None),
            P(("seq", "fsdp"), None),
            P(("seq", "fsdp"), None),
            P(("seq", "fsdp"), None),
            P(("seq", "fsdp"), None),
            P(("seq", "fsdp"), None),
            P(("seq", "fsdp"), None),
            P(("seq", "fsdp"), None),
            P(("seq", "fsdp"), None),
            P(("seq", "fsdp"), None),
            P(("seq", "fsdp"), None),
            P(("seq", "fsdp"), None),
            P(),
            P(),
            P(),
            P(),
            P(),
            P(),
        ),
        check_vma=False,
    )
```

```python
import functools

import jax
import jax.numpy as jnp
from jax import lax
from jax.experimental import pallas as pl
from jax.experimental.pallas import tpu as pltpu
from jax.sharding import PartitionSpec as P

D = 1024
QUERY_HEADS = 16
KEY_VALUE_HEADS = 8
HEAD_SIZE = 128
FF = 3072
QUERY_COLS = QUERY_HEADS * HEAD_SIZE
KEY_COLS = KEY_VALUE_HEADS * HEAD_SIZE

NORM_EPS = 1e-06
ROPE_THETA = 1000000.0
LEARN_RATE = 0.04
BETA_ONE = 0.9
BETA_TWO = 0.95
ADAM_EPS = 1e-08
WEIGHT_DECAY = 0.1
CLIP_NORM = 1.0
PRECISE = lax.Precision.HIGHEST
MASKED = -1e30
LOG2E = 1.4426950408889634
MESH = pl.DeviceIdType.MESH
VMEM_BYTES = 56 * 2**20


def rms_norm(values, gain_vec):
    return (
        values * lax.rsqrt(jnp.mean(values * values, axis=-1, keepdims=True) + NORM_EPS) * gain_vec
    )


def layout(bounds, token_pos):
    segment = jnp.sum((token_pos[:, None] >= bounds[None, :]).astype(jnp.int32), axis=1)
    starts_all = jnp.concatenate([jnp.zeros((1,), jnp.int32), bounds])
    slot_ids = jnp.arange(bounds.shape[0] + 1, dtype=jnp.int32)
    begin = jnp.sum(
        jnp.where(segment[:, None] == slot_ids[None, :], starts_all[None, :], 0), axis=1
    )
    return (segment, begin)


def exchange_kernel(n_seq, n_fsdp, to_all, x_ref, *refs):
    o_ref, send_sem, recv_sem, own_sem = refs[-4:]
    seq_at, fsdp_at = lax.axis_index("seq"), lax.axis_index("fsdp")
    count = n_seq * n_fsdp
    me = seq_at * n_fsdp + fsdp_at

    def place(step):
        other = lax.rem(me + step, count)
        return other, (other // n_fsdp, lax.rem(other, n_fsdp))

    barrier = pltpu.get_barrier_semaphore()

    def greet(step, carry):
        pl.semaphore_signal(barrier, inc=1, device_id=place(step)[1], device_id_type=MESH)
        return carry

    lax.fori_loop(1, count, greet, 0)
    pl.semaphore_wait(barrier, count - 1)
    own = pltpu.make_async_copy(x_ref if to_all else x_ref.at[me], o_ref.at[me], own_sem)
    own.start()

    def copy(step):
        other, where = place(step)
        return pltpu.make_async_remote_copy(
            src_ref=x_ref if to_all else x_ref.at[other],
            dst_ref=o_ref.at[me],
            send_sem=send_sem.at[step],
            recv_sem=recv_sem.at[step],
            device_id=where,
            device_id_type=MESH,
        )

    def begin(step, carry):
        copy(step).start()
        return carry

    def finish(step, carry):
        copy(step).wait()
        return carry

    lax.fori_loop(1, count, begin, 0)
    own.wait()
    lax.fori_loop(1, count, finish, 0)


def exchange(blocks, to_all, collective_id, after=()):
    n_seq, n_fsdp = lax.axis_size("seq"), lax.axis_size("fsdp")
    count = n_seq * n_fsdp
    shape = (count,) + blocks.shape if to_all else blocks.shape
    return pl.pallas_call(
        functools.partial(exchange_kernel, n_seq, n_fsdp, to_all),
        out_shape=jax.ShapeDtypeStruct(shape, blocks.dtype),
        in_specs=[pl.BlockSpec(memory_space=pl.ANY)] * (1 + len(after)),
        out_specs=pl.BlockSpec(memory_space=pl.ANY),
        scratch_shapes=[
            pltpu.SemaphoreType.DMA((count,)),
            pltpu.SemaphoreType.DMA((count,)),
            pltpu.SemaphoreType.DMA,
        ],
        compiler_params=pltpu.CompilerParams(collective_id=collective_id, has_side_effects=True),
    )(blocks, *after)


def sum_small(values, collective_id):
    rows = -(-values.shape[0] // 1024) * 8
    block = jnp.zeros((rows * 128,), jnp.float32).at[: values.shape[0]].set(values)
    parts = exchange(block.reshape(rows, 128), True, collective_id)
    return jnp.sum(parts, axis=0).reshape(-1)[: values.shape[0]]


def capacity(tokens, owners):
    return -(-(5 * tokens) // (4 * owners * 16)) * 16


def rank_ids(ids, height):
    at = jnp.arange(ids.shape[0], dtype=jnp.int32)
    again = jnp.any((ids[:, None] == ids[None, :]) & (at[None, :] < at[:, None]), axis=1)
    owner = ids // height
    floor = owner * height
    below = (
        (ids[None, :] < ids[:, None]) & (ids[None, :] >= floor[:, None]) & jnp.logical_not(again)[None, :]
    )
    return owner, jnp.sum(below.astype(jnp.int32), axis=1)


def slot_lists(ids, owner, rank, start, size, owners, height):
    within = rank - start
    valid = (within >= 0) & (within < size)
    slot = jnp.where(valid, owner * size + within, -1)
    slot_ids = jnp.arange(owners * size, dtype=jnp.int32)
    rows = jnp.max(
        jnp.where(slot[None, :] == slot_ids[:, None], (ids - owner * height)[None, :], -1), axis=1
    )
    return slot, rows.reshape(owners, size)


def pick_rows(table, wanted):
    count, size = wanted.shape
    rows = jnp.take(table, jnp.maximum(wanted, 0).reshape(-1), axis=0)
    return lax.optimization_barrier(rows).astype(jnp.bfloat16).reshape(count, size, table.shape[1])


def one_hot(slot, slots):
    return (slot[:, None] == jnp.arange(slots, dtype=jnp.int32)[None, :]).astype(jnp.bfloat16)


def spread_rows(arrived, slot, n_seq):
    count, size, columns = arrived.shape
    chosen = one_hot(slot, count // n_seq * size)
    parts = arrived.reshape(n_seq, -1, columns)
    return jnp.concatenate(
        [jnp.dot(chosen, parts[s], preferred_element_type=jnp.float32) for s in range(n_seq)], axis=1
    ).astype(jnp.bfloat16)


def collect_rows(token_grad, slot, n_seq, n_fsdp, size):
    chosen = one_hot(slot, n_fsdp * size)
    columns = token_grad.shape[1] // n_seq
    parts = [
        lax.dot_general(
            chosen,
            token_grad[:, s * columns : (s + 1) * columns],
            (((0,), (0,)), ((), ())),
            preferred_element_type=jnp.float32,
        )
        .astype(jnp.bfloat16)
        .reshape(n_fsdp, size, columns)
        for s in range(n_seq)
    ]
    return jnp.concatenate(parts, axis=0)


def embed_forward(token_ids, table):
    n_seq, n_fsdp = lax.axis_size("seq"), lax.axis_size("fsdp")
    ids = token_ids.reshape(-1)
    tokens, height = ids.shape[0], table.shape[0]
    size = capacity(tokens, n_fsdp)
    owner, rank = rank_ids(ids, height)
    slot, rows = slot_lists(ids, owner, rank, 0, size, n_fsdp, height)
    width = -(-(size + 1) // 1024) * 1024
    note = jnp.zeros((n_fsdp, width), jnp.int32)
    note = note.at[:, :size].set(rows).at[:, size].set(jnp.max(rank))
    note = note.reshape(n_fsdp, width // 128, 128)
    note = jnp.concatenate([note] * n_seq, axis=0)
    heard = exchange(note, False, 1).reshape(n_seq * n_fsdp, width)
    wanted = heard[:, :size]
    most = jnp.max(heard[:, size])
    arrived = exchange(pick_rows(table, wanted), False, 2)

    def plain(arrived):
        return spread_rows(arrived, slot, n_seq)

    def rounds(arrived):
        def another(carry):
            start, total = carry
            slot, rows = slot_lists(ids, owner, rank, start, size, n_fsdp, height)
            wanted = lax.all_to_all(
                jnp.concatenate([rows] * n_seq, axis=0), ("seq", "fsdp"), 0, 0, tiled=True
            )
            own_table = lax.optimization_barrier((table, start))[0]
            arrived = lax.all_to_all(pick_rows(own_table, wanted), ("seq", "fsdp"), 0, 0, tiled=True)
            return start + size, total + spread_rows(arrived, slot, n_seq)

        return lax.while_loop(lambda carry: carry[0] <= most, another, (jnp.int32(size), plain(arrived)))[1]

    embedded = lax.cond(most < size, plain, rounds, arrived)
    return embedded, (ids, owner, rank, slot, wanted, most, size)


def add_rows(total, arrived, wanted):
    height = total.shape[0]
    target = jnp.where(wanted >= 0, wanted, height).reshape(-1)
    rows = arrived.reshape(target.shape[0], -1).astype(jnp.float32)
    return total.at[target].add(rows, mode="drop")


def scatter_kernel(size, wanted_ref, count_ref, arrived_ref, *refs):
    total_ref, square_ref, rows_ref = refs[-3:]
    sources = arrived_ref.shape[0]
    height = total_ref.shape[0]

    def clear(i, carry):
        at = pl.ds(pl.multiple_of(i * 8, 8), 8)
        total_ref[at, :] = jnp.zeros((8, total_ref.shape[1]), jnp.float32)
        return carry

    whole = height // 8
    lax.fori_loop(0, whole, clear, 0, unroll=8)
    if height % 8:
        total_ref[whole * 8 :, :] = jnp.zeros((height % 8, total_ref.shape[1]), jnp.float32)

    def one_source(k, carry):
        rows_ref[...] = arrived_ref[k].astype(jnp.float32)
        count = count_ref[k]

        def four(i, inner):
            first = i * 4
            at = [wanted_ref[k * size + first + n] for n in range(4)]
            sums = [total_ref[pl.ds(at[n], 1), :] + rows_ref[pl.ds(first + n, 1), :] for n in range(4)]
            for n in range(4):
                total_ref[pl.ds(at[n], 1), :] = sums[n]
            return inner

        def one(i, inner):
            at = wanted_ref[k * size + i]
            total_ref[pl.ds(at, 1), :] += rows_ref[pl.ds(i, 1), :]
            return inner

        lax.fori_loop(0, count // 4, four, 0)
        lax.fori_loop(count // 4 * 4, count, one, 0)
        return carry

    lax.fori_loop(0, sources, one_source, 0)

    def add_square(i, carry):
        block = total_ref[pl.ds(pl.multiple_of(i * 8, 8), 8), :]
        return carry + block * block

    partial = lax.fori_loop(0, whole, add_square, jnp.zeros((8, total_ref.shape[1]), jnp.float32), unroll=8)
    if height % 8:
        rest = total_ref[whole * 8 :, :]
        partial = partial + jnp.concatenate(
            [rest * rest, jnp.zeros((8 - height % 8, total_ref.shape[1]), jnp.float32)], axis=0
        )
    square_ref[...] = partial


def scatter_rows(arrived, wanted, height, after):
    sources, size, width = arrived.shape
    counts = jnp.sum((wanted >= 0).astype(jnp.int32), axis=1)
    vmem = pl.BlockSpec(memory_space=pltpu.VMEM)
    return pl.pallas_call(
        functools.partial(scatter_kernel, size),
        grid_spec=pltpu.PrefetchScalarGridSpec(
            num_scalar_prefetch=2,
            grid=(),
            in_specs=[vmem] + [pl.BlockSpec(memory_space=pl.ANY)] * len(after),
            out_specs=[vmem, vmem],
            scratch_shapes=[pltpu.VMEM((size, width), jnp.float32)],
        ),
        out_shape=[
            jax.ShapeDtypeStruct((height, width), jnp.float32),
            jax.ShapeDtypeStruct((8, width), jnp.float32),
        ],
        compiler_params=pltpu.CompilerParams(vmem_limit_bytes=VMEM_BYTES),
        cost_estimate=pl.CostEstimate(flops=10**9, bytes_accessed=80 * 2**20, transcendentals=0),
    )(wanted.reshape(-1), counts, arrived, *after)


def embed_send(token_grad, kept):
    n_seq, n_fsdp = lax.axis_size("seq"), lax.axis_size("fsdp")
    slot, size = kept[3], kept[6]
    return lax.all_to_all(collect_rows(token_grad, slot, n_seq, n_fsdp, size), ("seq", "fsdp"), 0, 0, tiled=True)


def embed_backward(token_grad, arrived, kept, height, after):
    n_seq, n_fsdp = lax.axis_size("seq"), lax.axis_size("fsdp")
    ids, owner, rank, slot, wanted, most, size = kept

    def plain(arrived, *after):
        total, squares = scatter_rows(arrived, wanted, height, after)
        return total, jnp.sum(squares)

    def rounds(arrived, *after):
        def another(carry):
            start, total = carry
            slot, rows = slot_lists(ids, owner, rank, start, size, n_fsdp, height)
            wanted = lax.all_to_all(
                jnp.concatenate([rows] * n_seq, axis=0), ("seq", "fsdp"), 0, 0, tiled=True
            )
            arrived = lax.all_to_all(
                collect_rows(token_grad, slot, n_seq, n_fsdp, size), ("seq", "fsdp"), 0, 0, tiled=True
            )
            return start + size, add_rows(total, arrived, wanted)

        total = plain(arrived, *after)[0]
        total = lax.while_loop(lambda carry: carry[0] <= most, another, (jnp.int32(size), total))[1]
        return total, jnp.sum(total * total)

    return lax.cond(most < size, plain, rounds, arrived, *after)


ANY = pl.BlockSpec(memory_space=pl.ANY)
HALF = KEY_VALUE_HEADS // 2


def turn(values):
    return pltpu.roll(values, HEAD_SIZE // 2, axis=1)


def columns(head):
    return slice(head * HEAD_SIZE, (head + 1) * HEAD_SIZE)


def shape_head(raw, cosine, sine, gain):
    raw = raw.astype(jnp.float32)
    scale = lax.rsqrt(jnp.mean(raw * raw, axis=-1, keepdims=True) + NORM_EPS)
    normed = raw * scale * gain
    return (normed * cosine + turn(normed) * sine).astype(jnp.bfloat16)


def shape_head_back(raw, cosine, sine, gain, grad):
    raw = raw.astype(jnp.float32)
    scale = lax.rsqrt(jnp.mean(raw * raw, axis=-1, keepdims=True) + NORM_EPS)
    grad = grad * cosine + turn(grad * sine)
    unit = raw * scale
    gain_grad = jnp.sum(grad * unit, axis=0, keepdims=True)
    grad = grad * gain
    inner = jnp.mean(grad * unit, axis=-1, keepdims=True)
    return (scale * (grad - unit * inner)).astype(jnp.bfloat16), gain_grad


def queries_kernel(raw_ref, cos_ref, sin_ref, gain_ref, out_ref):
    for head in range(QUERY_HEADS):
        at = columns(head)
        out_ref[:, at] = shape_head(raw_ref[:, at], cos_ref[...], sin_ref[...], gain_ref[0:1, :])


def keys_kernel(raw_ref, cos_ref, sin_ref, gain_ref, *out_refs):
    for head in range(KEY_VALUE_HEADS):
        out_ref = out_refs[head // HALF]
        out_ref[:, columns(head % HALF)] = shape_head(
            raw_ref[:, columns(head)], cos_ref[...], sin_ref[...], gain_ref[1:2, :]
        )
    for half in range(2):
        first = KEY_COLS + half * HALF * HEAD_SIZE
        out_refs[half][:, HALF * HEAD_SIZE :] = raw_ref[:, first : first + HALF * HEAD_SIZE]


def token_blocks(rows, width):
    return pl.BlockSpec((rows, width), lambda i: (i, 0))


def shape_queries(raw, cosine, sine, gains):
    tokens = raw.shape[0]
    rows = min(256, tokens)
    return pl.pallas_call(
        queries_kernel,
        grid=(tokens // rows,),
        in_specs=[
            token_blocks(rows, QUERY_COLS),
            token_blocks(rows, HEAD_SIZE),
            token_blocks(rows, HEAD_SIZE),
            pl.BlockSpec((2, HEAD_SIZE), lambda i: (0, 0)),
        ],
        out_specs=token_blocks(rows, QUERY_COLS),
        out_shape=jax.ShapeDtypeStruct((tokens, QUERY_COLS), jnp.bfloat16),
        compiler_params=pltpu.CompilerParams(vmem_limit_bytes=VMEM_BYTES),
        cost_estimate=pl.CostEstimate(flops=4 * 10**9, bytes_accessed=8 * 2**20, transcendentals=0),
    )(raw, cosine, sine, gains)


def shape_keys(raw, cosine, sine, gains):
    tokens = raw.shape[0]
    rows = min(256, tokens)
    half = jax.ShapeDtypeStruct((tokens, KEY_COLS), jnp.bfloat16)
    return pl.pallas_call(
        keys_kernel,
        grid=(tokens // rows,),
        in_specs=[
            token_blocks(rows, 2 * KEY_COLS),
            token_blocks(rows, HEAD_SIZE),
            token_blocks(rows, HEAD_SIZE),
            pl.BlockSpec((2, HEAD_SIZE), lambda i: (0, 0)),
        ],
        out_specs=[token_blocks(rows, KEY_COLS)] * 2,
        out_shape=[half, half],
        compiler_params=pltpu.CompilerParams(vmem_limit_bytes=VMEM_BYTES),
        cost_estimate=pl.CostEstimate(flops=2 * 10**9, bytes_accessed=8 * 2**20, transcendentals=0),
    )(raw, cosine, sine, gains)


def add_gain_grad(gain_ref, total):
    @pl.when(pl.program_id(0) == 0)
    def _():
        gain_ref[...] = jnp.zeros_like(gain_ref)

    gain_ref[0:1, :] += total


def queries_back_kernel(raw_ref, cos_ref, sin_ref, gain_ref, dq_ref, *refs):
    out_ref, dgain_ref = refs[-2:]
    total = jnp.zeros((1, HEAD_SIZE), jnp.float32)
    for head in range(QUERY_HEADS):
        at = columns(head)
        grad = dq_ref[:, at].astype(jnp.float32)
        out_ref[:, at], part = shape_head_back(raw_ref[:, at], cos_ref[...], sin_ref[...], gain_ref[0:1, :], grad)
        total = total + part
    add_gain_grad(dgain_ref, total)


def keys_back_kernel(raw_ref, cos_ref, sin_ref, gain_ref, own_a_ref, own_b_ref, more_a_ref, more_b_ref, *refs):
    out_ref, dgain_ref = refs[-2:]
    total = jnp.zeros((1, HEAD_SIZE), jnp.float32)
    for head in range(KEY_VALUE_HEADS):
        own_ref, more_ref = ((own_a_ref, more_a_ref), (own_b_ref, more_b_ref))[head // HALF]
        at, part_at = columns(head), columns(head % HALF)
        grad = own_ref[0, :, part_at] + more_ref[0, :, part_at].astype(jnp.float32)
        out_ref[:, at], part = shape_head_back(raw_ref[:, at], cos_ref[...], sin_ref[...], gain_ref[1:2, :], grad)
        total = total + part
    for half, (own_ref, more_ref) in enumerate(((own_a_ref, more_a_ref), (own_b_ref, more_b_ref))):
        first = KEY_COLS + half * HALF * HEAD_SIZE
        out_ref[:, first : first + HALF * HEAD_SIZE] = (
            own_ref[1] + more_ref[1].astype(jnp.float32)
        ).astype(jnp.bfloat16)
    add_gain_grad(dgain_ref, total)


def shape_back(kernel, raw, cosine, sine, gains, grads, after=()):
    tokens = raw.shape[0]
    rows = min(128, tokens)
    wide = [
        pl.BlockSpec((2, rows, g.shape[2]), lambda i: (0, i, 0)) if g.ndim == 3 else token_blocks(rows, g.shape[1])
        for g in grads
    ]
    return pl.pallas_call(
        kernel,
        grid=(tokens // rows,),
        in_specs=[
            token_blocks(rows, raw.shape[1]),
            token_blocks(rows, HEAD_SIZE),
            token_blocks(rows, HEAD_SIZE),
            pl.BlockSpec((2, HEAD_SIZE), lambda i: (0, 0)),
        ]
        + wide
        + [ANY] * len(after),
        out_specs=[token_blocks(rows, raw.shape[1]), pl.BlockSpec((8, HEAD_SIZE), lambda i: (0, 0))],
        out_shape=[
            jax.ShapeDtypeStruct(raw.shape, jnp.bfloat16),
            jax.ShapeDtypeStruct((8, HEAD_SIZE), jnp.float32),
        ],
        compiler_params=pltpu.CompilerParams(vmem_limit_bytes=VMEM_BYTES),
        cost_estimate=pl.CostEstimate(flops=5 * 10**9, bytes_accessed=20 * 2**20, transcendentals=0),
    )(raw, cosine, sine, gains, *grads, *after)


def both_heads(block):
    return jnp.concatenate([block[:, :HEAD_SIZE], block[:, HEAD_SIZE:]], axis=0)


def key_ranges(scalar_ref, step, rows, keys):
    first_own, first_before, low = scalar_ref[0], scalar_ref[1], scalar_ref[2 + 2 * step]
    before = (jnp.minimum(low, first_own) - first_before) // keys, (first_own - first_before) // keys
    own = jnp.maximum(low - first_own, 0) // keys, ((step + 1) * rows - 1) // keys + 1
    return first_own, first_before, before, own


def allowed_keys(begin_ref, offset, rows, keys):
    begin = begin_ref[...] - offset
    at = lax.broadcasted_iota(jnp.int32, (rows, 1), 0)
    key_at = lax.broadcasted_iota(jnp.int32, (rows, keys), 1)
    return begin, at, key_at


def visit_blocks(scalar_ref, begin_ref, rows, keys, refs, work):
    step = pl.program_id(1)
    first_own, first_before, before, own = key_ranges(scalar_ref, step, rows, keys)
    first_row = first_own + step * rows
    last_begin = scalar_ref[3 + 2 * step]

    def run(bounds, base, group):
        def one(j, carry):
            at = pl.ds(pl.multiple_of(j * keys, keys), keys)
            first_key = base + j * keys
            whole = (first_key + keys - 1 <= first_row) & (first_key >= last_begin)

            @pl.when(whole)
            def _():
                work(*group, at, None)

            @pl.when(jnp.logical_not(whole))
            def _():
                begin = begin_ref[...] - first_key
                row = (first_row - first_key) + lax.broadcasted_iota(jnp.int32, (rows, 1), 0)
                key = lax.broadcasted_iota(jnp.int32, (rows, keys), 1)
                work(*group, at, (key <= row) & (key >= begin))

            return carry

        lax.fori_loop(bounds[0], bounds[1], one, 0)

    run(before, first_before, refs[0])
    run(own, first_own, refs[1])


def forward_kernel(keys, scalar_ref, q_ref, kb_ref, vb_ref, k_ref, v_ref, begin_ref, *refs):
    o_ref, lse_ref, acc_ref = refs[-3:]
    rows = q_ref.shape[0]
    query = both_heads(q_ref[...])
    acc_ref[...] = jnp.zeros_like(acc_ref)
    ones = jnp.ones((keys, HEAD_SIZE), jnp.bfloat16)

    def work(key_ref, value_ref, at, mask):
        value = jnp.concatenate([value_ref[at, :], ones], axis=1)
        scores = [
            lax.dot_general(
                query[h * rows : (h + 1) * rows], key_ref[at, :], (((1,), (1,)), ((), ())),
                preferred_element_type=jnp.float32,
            )
            for h in range(2)
        ]
        for h in range(2):
            weight = jnp.exp2(scores[h] * (LOG2E * HEAD_SIZE**-0.5))
            if mask is not None:
                weight = jnp.where(mask, weight, 0.0)
            acc_ref[h * rows : (h + 1) * rows, :] += jnp.dot(
                weight.astype(jnp.bfloat16), value, preferred_element_type=jnp.float32
            )

    visit_blocks(scalar_ref, begin_ref, rows, keys, ((kb_ref, vb_ref), (k_ref, v_ref)), work)
    acc = acc_ref[...]
    total = acc[:, HEAD_SIZE : HEAD_SIZE + 1]
    out = (acc[:, :HEAD_SIZE] / total).astype(jnp.bfloat16)
    o_ref[:, :HEAD_SIZE] = out[:rows]
    o_ref[:, HEAD_SIZE:] = out[rows:]
    lse = jnp.log2(total)
    lse_ref[0, :, 0:1] = lse[:rows]
    lse_ref[0, :, 1:2] = lse[rows:]


def attention_specs(tokens, length, rows, first):
    key = lambda h, i, s: (0, h)
    value = lambda h, i, s: (0, HALF + h)
    return [
        pl.BlockSpec((rows, 2 * HEAD_SIZE), lambda h, i, s: (i, first + h)),
        pl.BlockSpec((length, HEAD_SIZE), key),
        pl.BlockSpec((length, HEAD_SIZE), value),
        pl.BlockSpec((tokens, HEAD_SIZE), key),
        pl.BlockSpec((tokens, HEAD_SIZE), value),
        pl.BlockSpec((rows, 1), lambda h, i, s: (i, 0)),
    ]


def attention_forward(scalars, query, before, own, begin, rows, keys, first, filled):
    tokens = query.shape[0]
    specs = attention_specs(tokens, before.shape[0], rows, first)
    return pl.pallas_call(
        functools.partial(forward_kernel, keys),
        grid_spec=pltpu.PrefetchScalarGridSpec(
            num_scalar_prefetch=1,
            grid=(HALF, tokens // rows),
            in_specs=specs + [ANY] * len(filled),
            out_specs=[specs[0], pl.BlockSpec((1, rows, 2), lambda h, i, s: (first + h, i, 0))],
            scratch_shapes=[pltpu.VMEM((2 * rows, 2 * HEAD_SIZE), jnp.float32)],
        ),
        out_shape=[
            jax.ShapeDtypeStruct((tokens, QUERY_COLS), jnp.bfloat16),
            jax.ShapeDtypeStruct((KEY_VALUE_HEADS, tokens, 2), jnp.float32),
        ],
        input_output_aliases={7 + i: i for i in range(len(filled))},
        compiler_params=pltpu.CompilerParams(vmem_limit_bytes=VMEM_BYTES),
        cost_estimate=pl.CostEstimate(flops=20 * 10**9, bytes_accessed=16 * 2**20, transcendentals=10**7),
    )(scalars, query, before, before, own, own, begin, *filled)


def backward_kernel(keys, scalar_ref, q_ref, kb_ref, vb_ref, k_ref, v_ref, begin_ref, do_ref, o_ref, lse_ref, *refs):
    dq_ref, before_ref, own_ref, acc_ref, dq_acc_ref = refs[-5:]
    step = pl.program_id(1)
    rows = q_ref.shape[0]
    query = both_heads(q_ref[...])
    grad = both_heads(do_ref[...])
    out = both_heads(o_ref[...])
    lse = jnp.concatenate([lse_ref[0, :, 0:1], lse_ref[0, :, 1:2]], axis=0)
    inner = jnp.sum(grad.astype(jnp.float32) * out.astype(jnp.float32), axis=-1, keepdims=True)

    @pl.when(step == 0)
    def _():
        acc_ref[...] = jnp.zeros_like(acc_ref)
        own_ref[...] = jnp.zeros_like(own_ref)

    dq_acc_ref[...] = jnp.zeros_like(dq_acc_ref)

    def work(key_ref, value_ref, sum_ref, at, mask):
        key = key_ref[at, :]
        score = lax.dot_general(query, key, (((1,), (1,)), ((), ())), preferred_element_type=jnp.float32)
        prob_grad = lax.dot_general(
            grad, value_ref[at, :], (((1,), (1,)), ((), ())), preferred_element_type=jnp.float32
        )
        prob = jnp.exp2(score * (LOG2E * HEAD_SIZE**-0.5) - lse)
        if mask is not None:
            prob = jnp.where(jnp.concatenate([mask, mask], axis=0), prob, 0.0)
        sum_ref[1, at, :] += lax.dot_general(
            prob.astype(jnp.bfloat16), grad, (((0,), (0,)), ((), ())), preferred_element_type=jnp.float32
        )
        score_grad = (prob * (prob_grad - inner)).astype(jnp.bfloat16)
        sum_ref[0, at, :] += lax.dot_general(
            score_grad, query, (((0,), (0,)), ((), ())), preferred_element_type=jnp.float32
        )
        dq_acc_ref[...] += jnp.dot(score_grad, key, preferred_element_type=jnp.float32)

    visit_blocks(
        scalar_ref, begin_ref, rows, keys, ((kb_ref, vb_ref, acc_ref), (k_ref, v_ref, own_ref)), work
    )
    dq = dq_acc_ref[...] * HEAD_SIZE**-0.5
    dq_ref[:, :HEAD_SIZE] = dq[:rows]
    dq_ref[:, HEAD_SIZE:] = dq[rows:]

    @pl.when(step == pl.num_programs(1) - 1)
    def _():
        own_ref[0] = own_ref[0] * HEAD_SIZE**-0.5
        before_ref[0] = (acc_ref[0] * HEAD_SIZE**-0.5).astype(before_ref.dtype)
        before_ref[1] = acc_ref[1].astype(before_ref.dtype)


def attention_backward(scalars, query, before, own, begin, grad_out, out, lse, rows, keys, first, filled, after):
    tokens, length = query.shape[0], before.shape[0]
    specs = attention_specs(tokens, length, rows, first)
    both = lambda h, i, s: (0, 0, h)
    before_type = jnp.bfloat16 if length == tokens else jnp.float32
    return pl.pallas_call(
        functools.partial(backward_kernel, keys),
        grid_spec=pltpu.PrefetchScalarGridSpec(
            num_scalar_prefetch=1,
            grid=(HALF, tokens // rows),
            in_specs=specs
            + [specs[0], specs[0], pl.BlockSpec((1, rows, 2), lambda h, i, s: (first + h, i, 0))]
            + [ANY] * (len(filled) + len(after)),
            out_specs=[
                specs[0],
                pl.BlockSpec((2, length, HEAD_SIZE), both),
                pl.BlockSpec((2, tokens, HEAD_SIZE), both),
            ],
            scratch_shapes=[
                pltpu.VMEM((2, length, HEAD_SIZE), jnp.float32),
                pltpu.VMEM((2 * rows, HEAD_SIZE), jnp.float32),
            ],
        ),
        out_shape=[
            jax.ShapeDtypeStruct((tokens, QUERY_COLS), jnp.float32),
            jax.ShapeDtypeStruct((2, length, HALF * HEAD_SIZE), before_type),
            jax.ShapeDtypeStruct((2, tokens, HALF * HEAD_SIZE), jnp.float32),
        ],
        input_output_aliases={10 + i: i for i in range(len(filled))},
        compiler_params=pltpu.CompilerParams(vmem_limit_bytes=VMEM_BYTES),
        cost_estimate=pl.CostEstimate(flops=40 * 10**9, bytes_accessed=40 * 2**20, transcendentals=10**7),
    )(scalars, query, before, before, own, own, begin, grad_out, out, lse, *filled, *after)


def tokens_before(own):
    if lax.axis_size("seq") != 2:
        return lax.all_gather(own, "seq", axis=0, tiled=True)
    return lax.ppermute(own, "seq", [(0, 1), (1, 0)])


def to_tokens_before(parts):
    if lax.axis_size("seq") != 2:
        return lax.psum_scatter(parts, "seq", scatter_dimension=1, tiled=True)
    return lax.ppermute(parts, "seq", [(0, 1), (1, 0)])


def fetch(weight):
    return lax.all_gather(weight.astype(jnp.bfloat16), ("seq", "fsdp"), axis=0, tiled=True)


def trade(values, axis, bit):
    count = lax.axis_size(axis)
    return lax.ppermute(values, axis, [(i, i ^ bit) for i in range(count)])


def halves(values, dim, at):
    return (
        lax.dynamic_index_in_dim(values, at, dim, keepdims=False),
        lax.dynamic_index_in_dim(values, 1 - at, dim, keepdims=False),
    )


def by_stages():
    return (lax.axis_size("seq"), lax.axis_size("fsdp")) == (2, 16)


def where_am_i():
    at = lax.axis_index("fsdp")
    return lax.axis_index("seq"), at >> 2, (at >> 1) & 1, at & 1


def gradient_kernel(height, core_ref, left_ref, right_ref, *refs):
    keep_ref, send_ref, turned_ref = refs[-3:]

    @pl.when(pl.program_id(1) == 0)
    def _():
        turned_ref[...] = left_ref[...].T

    product = jnp.dot(turned_ref[...], right_ref[...], preferred_element_type=jnp.float32)
    even = core_ref[0] == 0
    for p in range(keep_ref.shape[0]):
        first = product[2 * p * height : (2 * p + 1) * height]
        second = product[(2 * p + 1) * height : (2 * p + 2) * height]
        keep_ref[p] = jnp.where(even, first, second).astype(jnp.bfloat16)
        send_ref[p] = jnp.where(even, second, first).astype(jnp.bfloat16)


def gradient_blocks(left, right, rows, place, packed_rows, filled):
    tokens, tall = left.shape
    height = tall // 32
    pairs = rows // (2 * height)
    out = jax.ShapeDtypeStruct((16, packed_rows, D), jnp.bfloat16)
    block = pl.BlockSpec((pairs, height, D), lambda i, j, s: (i, place(j), 0))
    return pl.pallas_call(
        functools.partial(gradient_kernel, height),
        grid_spec=pltpu.PrefetchScalarGridSpec(
            num_scalar_prefetch=1,
            grid=(tall // rows, right.shape[1] // D),
            in_specs=[
                pl.BlockSpec((tokens, rows), lambda i, j, s: (0, i)),
                pl.BlockSpec((tokens, D), lambda i, j, s: (0, j)),
            ]
            + [ANY] * len(filled),
            out_specs=[block, block],
            scratch_shapes=[pltpu.VMEM((rows, tokens), jnp.bfloat16)],
        ),
        out_shape=[out, out],
        input_output_aliases={3 + i: i for i in range(len(filled))},
        compiler_params=pltpu.CompilerParams(vmem_limit_bytes=VMEM_BYTES),
        cost_estimate=pl.CostEstimate(
            flops=2 * tokens * tall * right.shape[1], bytes_accessed=16 * 2**20, transcendentals=0
        ),
    )(where_am_i()[3].reshape(1), left, right, *filled)


def core_kernel(at_ref, keep_ref, got_ref, *refs):
    left_keep_ref, left_send_ref, right_keep_ref, right_send_ref = refs[-4:]
    y_other, x_other = pl.program_id(0), pl.program_id(1)
    total = keep_ref[0] + got_ref[0]
    left, right = total[:, : D // 2], total[:, D // 2 :]

    @pl.when(y_other == 0)
    def _():
        left_keep_ref[0, 0] = left

    @pl.when(y_other == 1)
    def _():
        left_send_ref[0, 0] = left

    @pl.when(x_other == 0)
    def _():
        right_keep_ref[0, 0] = right

    @pl.when(x_other == 1)
    def _():
        right_send_ref[0, 0] = right


def sum_core(keep, send, after=()):
    rows = keep.shape[1]
    got = trade(send, "fsdp", 1)
    y_at, _, x_at, _ = where_am_i()

    def chip(a, b, z, s):
        return (((a ^ s[0]) * 4 + z) * 2 + (b ^ s[1]), 0, 0)

    def left_keep(a, b, z, s):
        return (jnp.where(a == 0, z, 3), jnp.where(a == 0, b, 1) ^ s[1], 0, 0)

    def left_send(a, b, z, s):
        return (jnp.where(a == 1, z, 0), jnp.where(a == 1, b, 0) ^ s[1], 0, 0)

    def right_keep(a, b, z, s):
        return (a ^ s[0], jnp.where(b == 0, z, 3), 0, 0)

    def right_send(a, b, z, s):
        return (jnp.where(b == 1, a, 0) ^ s[0], jnp.where(b == 1, z, jnp.where(a == 0, 0, 3)), 0, 0)

    full = pl.BlockSpec((1, rows, D), chip)
    part = lambda index: pl.BlockSpec((1, 1, rows, D // 2), index)
    left = jax.ShapeDtypeStruct((4, 2, rows, D // 2), jnp.bfloat16)
    right = jax.ShapeDtypeStruct((2, 4, rows, D // 2), jnp.bfloat16)
    lk, ls, rk, rs = pl.pallas_call(
        core_kernel,
        grid_spec=pltpu.PrefetchScalarGridSpec(
            num_scalar_prefetch=1,
            grid=(2, 2, 4),
            in_specs=[full, full] + [ANY] * len(after),
            out_specs=[part(left_keep), part(left_send), part(right_keep), part(right_send)],
        ),
        out_shape=[left, left, right, right],
        compiler_params=pltpu.CompilerParams(vmem_limit_bytes=VMEM_BYTES),
        cost_estimate=pl.CostEstimate(flops=10**9, bytes_accessed=96 * 2**10 * rows, transcendentals=0),
    )(jnp.stack([y_at, x_at]), keep, got, *after)
    return (lk, rk), (ls, rs)


def sum_first(keep, send):
    y_at, _, x_at, _ = where_am_i()
    low, wide = jnp.bfloat16, jnp.float32
    left = keep[0].astype(wide) + trade(send[0], "seq", 1).astype(wide)
    right = keep[1].astype(wide) + trade(send[1], "fsdp", 2).astype(wide)
    left_keep, left_send = halves(left, 1, x_at)
    right_keep, right_send = halves(right, 0, y_at)
    return (left_keep, right_keep), (left_send.astype(low), right_send.astype(low))


def sum_second(keep, send):
    z_at = where_am_i()[1]
    left = keep[0] + trade(send[0], "fsdp", 2).astype(jnp.float32)
    right = keep[1] + trade(send[1], "seq", 1).astype(jnp.float32)
    total = jnp.concatenate([left, right], axis=-1)
    own = lax.dynamic_index_in_dim(total, z_at, 0, keepdims=False)
    sends = tuple(
        lax.dynamic_index_in_dim(total, z_at ^ other, 0, keepdims=False).astype(jnp.bfloat16) for other in (1, 2, 3)
    )
    return own, sends


def sum_last(keep, send):
    total = keep
    for other in (1, 2, 3):
        total = total + trade(send[other - 1], "fsdp", 4 * other).astype(jnp.float32)
    return total


def beside(total, height, starts):
    return jnp.concatenate([total[r : r + height] for r in starts], axis=1)


def plain_sum(left, right):
    grad = lax.dot_general(left, right, (((0,), (0,)), ((), ())), preferred_element_type=jnp.float32)
    return lax.psum_scatter(grad, ("seq", "fsdp"), scatter_dimension=0, tiled=True)


def adam_update(weight, moment_one, moment_two, grad, factor, step_float):
    grad = grad * factor
    moment_one = BETA_ONE * moment_one + (1.0 - BETA_ONE) * grad
    moment_two = BETA_TWO * moment_two + (1.0 - BETA_TWO) * grad * grad
    fix_one = 1.0 - BETA_ONE**step_float
    fix_two = 1.0 - BETA_TWO**step_float
    weight = weight - LEARN_RATE * (
        moment_one / fix_one / (jnp.sqrt(moment_two / fix_two) + ADAM_EPS) + WEIGHT_DECAY * weight
    )
    return (weight, moment_one, moment_two)


def body(
    token_ids,
    seq_lengths,
    pairing,
    step_count,
    embedding,
    embedding_one,
    embedding_two,
    qkv_weight,
    qkv_one,
    qkv_two,
    out_weight,
    out_one,
    out_two,
    gate_up_weight,
    gate_up_one,
    gate_up_two,
    down_weight,
    down_one,
    down_two,
    norm_gains,
    gains_one,
    gains_two,
    score_weight,
    score_one,
    score_two,
):
    seq_at = lax.axis_index("seq")
    group_at = lax.axis_index("fsdp")
    token_rows = token_ids.shape[1]
    per_group = seq_lengths.shape[1] - 1
    lengths = seq_lengths[0]
    bounds = jnp.stack([jnp.sum(lengths[: j + 1]) for j in range(per_group)])
    token_pos = seq_at * token_rows + jnp.arange(token_rows, dtype=jnp.int32)
    segment, begin = layout(bounds, token_pos)
    frequency = ROPE_THETA ** (
        -2.0 * jnp.arange(HEAD_SIZE // 2, dtype=jnp.float32) / HEAD_SIZE
    )
    angles = (token_pos - begin).astype(jnp.float32)[:, None] * frequency[None, :]
    cosine, sine = jnp.cos(angles), jnp.sin(angles)
    cosine = jnp.concatenate([cosine, cosine], axis=1)
    sine = jnp.concatenate([-sine, sine], axis=1)
    query_rows = min(512, token_rows)
    key_rows = min(512, token_rows)
    begin_column = begin[:, None]
    attn_gain = norm_gains[:D]
    mlp_gain = norm_gains[D : 2 * D]
    final_gain = norm_gains[2 * D : 3 * D]
    head_gains = norm_gains[3 * D :].reshape(2, HEAD_SIZE)
    first_own = seq_at * token_rows
    first_before = first_own - token_rows if lax.axis_size("seq") == 2 else 0 * first_own
    scalars = jnp.concatenate(
        [
            jnp.stack([first_own, first_before]),
            jnp.stack([begin[::query_rows], begin[query_rows - 1 :: query_rows]], axis=1).reshape(-1),
        ]
    )
    qkv_full = fetch(qkv_weight)
    out_full, gate_up_full, down_full = fetch(out_weight), fetch(gate_up_weight), fetch(down_weight)
    embedded, kept = embed_forward(token_ids, embedding)
    resid_in = embedded.astype(jnp.float32)
    normed_low = rms_norm(resid_in, attn_gain).astype(jnp.bfloat16)
    key_value_raw = jnp.dot(
        normed_low, qkv_full[:, QUERY_COLS:], preferred_element_type=jnp.float32
    ).astype(jnp.bfloat16)
    own_a, own_b = shape_keys(key_value_raw, cosine, sine, head_gains)
    before_a, before_b = tokens_before(own_a), tokens_before(own_b)
    query_raw = jnp.dot(
        normed_low, qkv_full[:, :QUERY_COLS], preferred_element_type=jnp.float32
    ).astype(jnp.bfloat16)
    query_low = shape_queries(query_raw, cosine, sine, head_gains)
    results = attention_forward(
        scalars, query_low, before_a, own_a, begin_column, query_rows, key_rows, 0, ()
    )
    merged, lse = attention_forward(
        scalars, query_low, before_b, own_b, begin_column, query_rows, key_rows, HALF, tuple(results)
    )
    resid_mid = resid_in + jnp.dot(merged, out_full, preferred_element_type=jnp.float32)
    normed_two = rms_norm(resid_mid, mlp_gain).astype(jnp.bfloat16)
    gate_up = jnp.dot(normed_two, gate_up_full, preferred_element_type=jnp.float32)
    activated = (jax.nn.silu(gate_up[:, :FF]) * gate_up[:, FF:]).astype(jnp.bfloat16)
    resid_out = resid_mid + jnp.dot(activated, down_full, preferred_element_type=jnp.float32)
    final = rms_norm(resid_out, final_gain)
    per_token = jnp.sum(final * score_weight, axis=1)
    slot_list = jnp.arange(per_group, dtype=jnp.int32)
    seq_size = seq_lengths[0, :per_group].astype(jnp.float32)
    picker = (segment[None, :] == slot_list[:, None]).astype(jnp.float32) / seq_size[:, None]
    own_scores = jnp.sum(picker * per_token[None, :], axis=1)
    seq_total = pairing.shape[0]
    score_board = lax.dynamic_update_slice(
        jnp.zeros((seq_total,), jnp.float32), own_scores, (group_at * per_group,)
    )
    all_scores = sum_small(score_board, 3)
    pair_table = pairing.reshape(-1, 2)
    seq_ids = jnp.arange(seq_total, dtype=jnp.int32)
    choose = (pair_table[:, 0:1] == seq_ids[None, :]).astype(jnp.float32)
    reject = (pair_table[:, 1:2] == seq_ids[None, :]).astype(jnp.float32)
    margin = jnp.sum((choose - reject) * all_scores[None, :], axis=1)
    ranking_loss = jnp.sum(jax.nn.softplus(-margin))
    margin_grad = -jax.nn.sigmoid(-margin)
    score_grads = jnp.sum(margin_grad[:, None] * (choose - reject), axis=0)
    own_grads = lax.dynamic_slice_in_dim(score_grads, group_at * per_group, per_group)
    token_grad = jnp.sum(own_grads[:, None] * picker, axis=0)
    score_part = jnp.sum(token_grad[:, None] * final, axis=0)
    final_grad = token_grad[:, None] * score_weight[None, :]
    final_back = jax.vjp(rms_norm, resid_out, final_gain)[1]
    dresid_out, dfinal_gain = final_back(final_grad)
    mlp_low = dresid_out.astype(jnp.bfloat16)
    staged = by_stages()
    keep, send = (), ()
    if staged:
        early = gradient_blocks(activated, mlp_low, 768, lambda j: 0, 288, ())
    else:
        down_shard = plain_sum(activated, mlp_low)
    act_grad = jnp.dot(mlp_low, down_full.T, preferred_element_type=jnp.float32)
    act_back = jax.vjp(lambda joined: jax.nn.silu(joined[:, :FF]) * joined[:, FF:], gate_up)[1]
    gate_up_low = act_back(act_grad)[0].astype(jnp.bfloat16)
    if staged:
        early = gradient_blocks(normed_two, gate_up_low, 512, lambda j: 3 + j, 288, tuple(early))
    else:
        gate_up_shard = plain_sum(normed_two, gate_up_low)
    normed_two_grad = jnp.dot(gate_up_low, gate_up_full.T, preferred_element_type=jnp.float32)
    mid_back = jax.vjp(rms_norm, resid_mid, mlp_gain)[1]
    mid_extra, dmlp_gain = mid_back(normed_two_grad)
    dresid_mid = dresid_out + mid_extra
    attn_low = dresid_mid.astype(jnp.bfloat16)
    if staged:
        late = gradient_blocks(merged, attn_low, 512, lambda j: 0, 192, ())
        keep, send = sum_core(*early, (attn_low,))
    else:
        out_shard = plain_sum(merged, attn_low)
    merged_grad = jnp.dot(attn_low, out_full.T, preferred_element_type=jnp.float32).astype(
        jnp.bfloat16
    )
    common = (begin_column, merged_grad, merged, lse, query_rows, key_rows)
    query_grad, before_grad_a, own_grad_a = attention_backward(
        scalars, query_low, before_a, own_a, *common, 0, (), send
    )
    more_a = to_tokens_before(before_grad_a)
    if staged:
        keep, send = sum_first(keep, send)
    query_grad, before_grad_b, own_grad_b = attention_backward(
        scalars, query_low, before_b, own_b, *common, HALF, (query_grad,), send
    )
    more_b = to_tokens_before(before_grad_b)
    if staged:
        keep, send = sum_second(keep, send)
    query_raw_grad, query_sums = shape_back(
        queries_back_kernel, query_raw, cosine, sine, head_gains, (query_grad,), send
    )
    total = sum_last(keep, send) if staged else begin_column
    key_value_raw_grad, key_sums = shape_back(
        keys_back_kernel, key_value_raw, cosine, sine, head_gains, (own_grad_a, own_grad_b, more_a, more_b), (total,)
    )
    if staged:
        down_shard = total[:96]
        gate_up_shard = beside(total, 32, range(96, 288, 32))
        late = gradient_blocks(normed_low, query_raw_grad, 512, lambda j: 2 + j, 192, tuple(late))
        late = gradient_blocks(normed_low, key_value_raw_grad, 512, lambda j: 4 + j, 192, tuple(late))
        keep, send = sum_core(*late)
    else:
        send = ()
        qkv_shard = jnp.concatenate(
            [plain_sum(normed_low, query_raw_grad), plain_sum(normed_low, key_value_raw_grad)], axis=1
        )
    normed_grad = jnp.dot(
        query_raw_grad, qkv_full[:, :QUERY_COLS].T, preferred_element_type=jnp.float32
    ) + jnp.dot(key_value_raw_grad, qkv_full[:, QUERY_COLS:].T, preferred_element_type=jnp.float32)
    in_back = jax.vjp(rms_norm, resid_in, attn_gain)[1]
    in_extra, dattn_gain = in_back(normed_grad)
    dresid_in = dresid_mid + in_extra
    token_grad_low = dresid_in.astype(jnp.bfloat16)
    arrived = embed_send(token_grad_low, kept)
    if staged:
        keep, send = sum_first(keep, send)
        keep, send = sum_second(keep, send)
    embed_grad, square = embed_backward(token_grad_low, arrived, kept, embedding.shape[0], send)
    if staged:
        total = sum_last(keep, send)
        out_shard, qkv_shard = total[:64], beside(total, 32, range(64, 192, 32))
    shards = (qkv_shard, out_shard, gate_up_shard, down_shard)
    for shard in shards:
        square = square + jnp.sum(shard * shard)
    gain_part = jnp.concatenate([dattn_gain, dmlp_gain, dfinal_gain, query_sums[0], key_sums[0]])
    gain_count = gain_part.shape[0]
    sums = sum_small(jnp.concatenate([gain_part, score_part, square.reshape(1)]), 4)
    gain_sum, score_sum, square_sum = sums[:gain_count], sums[gain_count:-1], sums[-1]
    grad_norm = jnp.sqrt(square_sum + jnp.sum(gain_sum * gain_sum) + jnp.sum(score_sum * score_sum))
    factor = CLIP_NORM / jnp.maximum(grad_norm, CLIP_NORM)
    step_float = step_count[0]
    e_new = adam_update(embedding, embedding_one, embedding_two, embed_grad, factor, step_float)
    q_new = adam_update(qkv_weight, qkv_one, qkv_two, shards[0], factor, step_float)
    o_new = adam_update(out_weight, out_one, out_two, shards[1], factor, step_float)
    g_new = adam_update(gate_up_weight, gate_up_one, gate_up_two, shards[2], factor, step_float)
    d_new = adam_update(down_weight, down_one, down_two, shards[3], factor, step_float)
    n_new = adam_update(norm_gains, gains_one, gains_two, gain_sum, factor, step_float)
    s_new = adam_update(score_weight, score_one, score_two, score_sum, factor, step_float)
    clipped_gains = gain_sum * factor
    return (
        ranking_loss,
        grad_norm,
        e_new[0],
        e_new[1],
        e_new[2],
        q_new[0],
        q_new[1],
        q_new[2],
        o_new[0],
        o_new[1],
        o_new[2],
        g_new[0],
        g_new[1],
        g_new[2],
        d_new[0],
        d_new[1],
        d_new[2],
        clipped_gains,
        n_new[1],
        n_new[2],
        s_new[0],
        s_new[1],
        s_new[2],
    )


def solution(mesh):
    return jax.shard_map(
        body,
        mesh=mesh,
        in_specs=(
            P("fsdp", "seq"),
            P("fsdp", None),
            P(),
            P(),
            P("fsdp", "seq"),
            P("fsdp", "seq"),
            P("fsdp", "seq"),
            P(("seq", "fsdp"), None),
            P(("seq", "fsdp"), None),
            P(("seq", "fsdp"), None),
            P(("seq", "fsdp"), None),
            P(("seq", "fsdp"), None),
            P(("seq", "fsdp"), None),
            P(("seq", "fsdp"), None),
            P(("seq", "fsdp"), None),
            P(("seq", "fsdp"), None),
            P(("seq", "fsdp"), None),
            P(("seq", "fsdp"), None),
            P(("seq", "fsdp"), None),
            P(),
            P(),
            P(),
            P(),
            P(),
            P(),
        ),
        out_specs=(
            P(),
            P(),
            P("fsdp", "seq"),
            P("fsdp", "seq"),
            P("fsdp", "seq"),
            P(("seq", "fsdp"), None),
            P(("seq", "fsdp"), None),
            P(("seq", "fsdp"), None),
            P(("seq", "fsdp"), None),
            P(("seq", "fsdp"), None),
            P(("seq", "fsdp"), None),
            P(("seq", "fsdp"), None),
            P(("seq", "fsdp"), None),
            P(("seq", "fsdp"), None),
            P(("seq", "fsdp"), None),
            P(("seq", "fsdp"), None),
            P(("seq", "fsdp"), None),
            P(),
            P(),
            P(),
            P(),
            P(),
            P(),
        ),
        check_vma=False,
    )
```

```python
import functools

import jax
import jax.numpy as jnp
from jax import lax
from jax.experimental import pallas as pl
from jax.experimental.pallas import tpu as pltpu
from jax.sharding import PartitionSpec as P

D = 1024
QUERY_HEADS = 16
KEY_VALUE_HEADS = 8
HEAD_SIZE = 128
FF = 3072
QUERY_COLS = QUERY_HEADS * HEAD_SIZE
KEY_COLS = KEY_VALUE_HEADS * HEAD_SIZE

NORM_EPS = 1e-06
ROPE_THETA = 1000000.0
LEARN_RATE = 0.04
BETA_ONE = 0.9
BETA_TWO = 0.95
ADAM_EPS = 1e-08
WEIGHT_DECAY = 0.1
CLIP_NORM = 1.0
PRECISE = lax.Precision.HIGHEST
MASKED = -1e30
LOG2E = 1.4426950408889634
MESH = pl.DeviceIdType.MESH
VMEM_BYTES = 56 * 2**20


def rms_norm(values, gain_vec):
    return (
        values * lax.rsqrt(jnp.mean(values * values, axis=-1, keepdims=True) + NORM_EPS) * gain_vec
    )


def layout(bounds, token_pos):
    segment = jnp.sum((token_pos[:, None] >= bounds[None, :]).astype(jnp.int32), axis=1)
    starts_all = jnp.concatenate([jnp.zeros((1,), jnp.int32), bounds])
    slot_ids = jnp.arange(bounds.shape[0] + 1, dtype=jnp.int32)
    begin = jnp.sum(
        jnp.where(segment[:, None] == slot_ids[None, :], starts_all[None, :], 0), axis=1
    )
    return (segment, begin)


def exchange_kernel(n_seq, n_fsdp, to_all, x_ref, *refs):
    o_ref, send_sem, recv_sem, own_sem = refs[-4:]
    seq_at, fsdp_at = lax.axis_index("seq"), lax.axis_index("fsdp")
    count = n_seq * n_fsdp
    me = seq_at * n_fsdp + fsdp_at

    def place(step):
        other = lax.rem(me + step, count)
        return other, (other // n_fsdp, lax.rem(other, n_fsdp))

    barrier = pltpu.get_barrier_semaphore()

    def greet(step, carry):
        pl.semaphore_signal(barrier, inc=1, device_id=place(step)[1], device_id_type=MESH)
        return carry

    lax.fori_loop(1, count, greet, 0)
    pl.semaphore_wait(barrier, count - 1)
    own = pltpu.make_async_copy(x_ref if to_all else x_ref.at[me], o_ref.at[me], own_sem)
    own.start()

    def copy(step):
        other, where = place(step)
        return pltpu.make_async_remote_copy(
            src_ref=x_ref if to_all else x_ref.at[other],
            dst_ref=o_ref.at[me],
            send_sem=send_sem.at[step],
            recv_sem=recv_sem.at[step],
            device_id=where,
            device_id_type=MESH,
        )

    def begin(step, carry):
        copy(step).start()
        return carry

    def finish(step, carry):
        copy(step).wait()
        return carry

    lax.fori_loop(1, count, begin, 0)
    own.wait()
    lax.fori_loop(1, count, finish, 0)


def exchange(blocks, to_all, collective_id, after=()):
    n_seq, n_fsdp = lax.axis_size("seq"), lax.axis_size("fsdp")
    count = n_seq * n_fsdp
    shape = (count,) + blocks.shape if to_all else blocks.shape
    return pl.pallas_call(
        functools.partial(exchange_kernel, n_seq, n_fsdp, to_all),
        out_shape=jax.ShapeDtypeStruct(shape, blocks.dtype),
        in_specs=[pl.BlockSpec(memory_space=pl.ANY)] * (1 + len(after)),
        out_specs=pl.BlockSpec(memory_space=pl.ANY),
        scratch_shapes=[
            pltpu.SemaphoreType.DMA((count,)),
            pltpu.SemaphoreType.DMA((count,)),
            pltpu.SemaphoreType.DMA,
        ],
        compiler_params=pltpu.CompilerParams(collective_id=collective_id, has_side_effects=True),
    )(blocks, *after)


def sum_small(values, collective_id):
    rows = -(-values.shape[0] // 1024) * 8
    block = jnp.zeros((rows * 128,), jnp.float32).at[: values.shape[0]].set(values)
    parts = exchange(block.reshape(rows, 128), True, collective_id)
    return jnp.sum(parts, axis=0).reshape(-1)[: values.shape[0]]


def capacity(tokens, owners):
    return -(-(5 * tokens) // (4 * owners * 16)) * 16


def rank_ids(ids, height):
    at = jnp.arange(ids.shape[0], dtype=jnp.int32)
    again = jnp.any((ids[:, None] == ids[None, :]) & (at[None, :] < at[:, None]), axis=1)
    owner = ids // height
    floor = owner * height
    below = (
        (ids[None, :] < ids[:, None]) & (ids[None, :] >= floor[:, None]) & jnp.logical_not(again)[None, :]
    )
    return owner, jnp.sum(below.astype(jnp.int32), axis=1)


def slot_lists(ids, owner, rank, start, size, owners, height):
    within = rank - start
    valid = (within >= 0) & (within < size)
    slot = jnp.where(valid, owner * size + within, -1)
    slot_ids = jnp.arange(owners * size, dtype=jnp.int32)
    rows = jnp.max(
        jnp.where(slot[None, :] == slot_ids[:, None], (ids - owner * height)[None, :], -1), axis=1
    )
    return slot, rows.reshape(owners, size)


def pick_rows(table, wanted):
    count, size = wanted.shape
    rows = jnp.take(table, jnp.maximum(wanted, 0).reshape(-1), axis=0)
    return lax.optimization_barrier(rows).astype(jnp.bfloat16).reshape(count, size, table.shape[1])


def one_hot(slot, slots):
    return (slot[:, None] == jnp.arange(slots, dtype=jnp.int32)[None, :]).astype(jnp.bfloat16)


def spread_rows(arrived, slot, n_seq):
    count, size, columns = arrived.shape
    chosen = one_hot(slot, count // n_seq * size)
    parts = arrived.reshape(n_seq, -1, columns)
    return jnp.concatenate(
        [jnp.dot(chosen, parts[s], preferred_element_type=jnp.float32) for s in range(n_seq)], axis=1
    ).astype(jnp.bfloat16)


def collect_rows(token_grad, slot, n_seq, n_fsdp, size):
    chosen = one_hot(slot, n_fsdp * size)
    columns = token_grad.shape[1] // n_seq
    parts = [
        lax.dot_general(
            chosen,
            token_grad[:, s * columns : (s + 1) * columns],
            (((0,), (0,)), ((), ())),
            preferred_element_type=jnp.float32,
        )
        .astype(jnp.bfloat16)
        .reshape(n_fsdp, size, columns)
        for s in range(n_seq)
    ]
    return jnp.concatenate(parts, axis=0)


def embed_forward(token_ids, table):
    n_seq, n_fsdp = lax.axis_size("seq"), lax.axis_size("fsdp")
    ids = token_ids.reshape(-1)
    tokens, height = ids.shape[0], table.shape[0]
    size = capacity(tokens, n_fsdp)
    owner, rank = rank_ids(ids, height)
    slot, rows = slot_lists(ids, owner, rank, 0, size, n_fsdp, height)
    width = -(-(size + 1) // 1024) * 1024
    note = jnp.zeros((n_fsdp, width), jnp.int32)
    note = note.at[:, :size].set(rows).at[:, size].set(jnp.max(rank))
    note = note.reshape(n_fsdp, width // 128, 128)
    note = jnp.concatenate([note] * n_seq, axis=0)
    heard = exchange(note, False, 1).reshape(n_seq * n_fsdp, width)
    wanted = heard[:, :size]
    most = jnp.max(heard[:, size])
    arrived = exchange(pick_rows(table, wanted), False, 2)

    def plain(arrived):
        return spread_rows(arrived, slot, n_seq)

    def rounds(arrived):
        def another(carry):
            start, total = carry
            slot, rows = slot_lists(ids, owner, rank, start, size, n_fsdp, height)
            wanted = lax.all_to_all(
                jnp.concatenate([rows] * n_seq, axis=0), ("seq", "fsdp"), 0, 0, tiled=True
            )
            own_table = lax.optimization_barrier((table, start))[0]
            arrived = lax.all_to_all(pick_rows(own_table, wanted), ("seq", "fsdp"), 0, 0, tiled=True)
            return start + size, total + spread_rows(arrived, slot, n_seq)

        return lax.while_loop(lambda carry: carry[0] <= most, another, (jnp.int32(size), plain(arrived)))[1]

    embedded = lax.cond(most < size, plain, rounds, arrived)
    return embedded, (ids, owner, rank, slot, wanted, most, size)


def add_rows(total, arrived, wanted):
    height = total.shape[0]
    target = jnp.where(wanted >= 0, wanted, height).reshape(-1)
    rows = arrived.reshape(target.shape[0], -1).astype(jnp.float32)
    return total.at[target].add(rows, mode="drop")


def scatter_kernel(size, wanted_ref, count_ref, arrived_ref, *refs):
    total_ref, square_ref, rows_ref = refs[-3:]
    sources = arrived_ref.shape[0]
    height = total_ref.shape[0]

    def clear(i, carry):
        at = pl.ds(pl.multiple_of(i * 8, 8), 8)
        total_ref[at, :] = jnp.zeros((8, total_ref.shape[1]), jnp.float32)
        return carry

    whole = height // 8
    lax.fori_loop(0, whole, clear, 0, unroll=8)
    if height % 8:
        total_ref[whole * 8 :, :] = jnp.zeros((height % 8, total_ref.shape[1]), jnp.float32)

    def one_source(k, carry):
        rows_ref[...] = arrived_ref[k].astype(jnp.float32)
        count = count_ref[k]

        def four(i, inner):
            first = i * 4
            at = [wanted_ref[k * size + first + n] for n in range(4)]
            sums = [total_ref[pl.ds(at[n], 1), :] + rows_ref[pl.ds(first + n, 1), :] for n in range(4)]
            for n in range(4):
                total_ref[pl.ds(at[n], 1), :] = sums[n]
            return inner

        def one(i, inner):
            at = wanted_ref[k * size + i]
            total_ref[pl.ds(at, 1), :] += rows_ref[pl.ds(i, 1), :]
            return inner

        lax.fori_loop(0, count // 4, four, 0)
        lax.fori_loop(count // 4 * 4, count, one, 0)
        return carry

    lax.fori_loop(0, sources, one_source, 0)

    def add_square(i, carry):
        block = total_ref[pl.ds(pl.multiple_of(i * 8, 8), 8), :]
        return carry + block * block

    partial = lax.fori_loop(0, whole, add_square, jnp.zeros((8, total_ref.shape[1]), jnp.float32), unroll=8)
    if height % 8:
        rest = total_ref[whole * 8 :, :]
        partial = partial + jnp.concatenate(
            [rest * rest, jnp.zeros((8 - height % 8, total_ref.shape[1]), jnp.float32)], axis=0
        )
    square_ref[...] = partial


def scatter_rows(arrived, wanted, height, after):
    sources, size, width = arrived.shape
    counts = jnp.sum((wanted >= 0).astype(jnp.int32), axis=1)
    vmem = pl.BlockSpec(memory_space=pltpu.VMEM)
    return pl.pallas_call(
        functools.partial(scatter_kernel, size),
        grid_spec=pltpu.PrefetchScalarGridSpec(
            num_scalar_prefetch=2,
            grid=(),
            in_specs=[vmem] + [pl.BlockSpec(memory_space=pl.ANY)] * len(after),
            out_specs=[vmem, vmem],
            scratch_shapes=[pltpu.VMEM((size, width), jnp.float32)],
        ),
        out_shape=[
            jax.ShapeDtypeStruct((height, width), jnp.float32),
            jax.ShapeDtypeStruct((8, width), jnp.float32),
        ],
        compiler_params=pltpu.CompilerParams(vmem_limit_bytes=VMEM_BYTES),
        cost_estimate=pl.CostEstimate(flops=10**9, bytes_accessed=80 * 2**20, transcendentals=0),
    )(wanted.reshape(-1), counts, arrived, *after)


def embed_send(token_grad, kept):
    n_seq, n_fsdp = lax.axis_size("seq"), lax.axis_size("fsdp")
    slot, size = kept[3], kept[6]
    return lax.all_to_all(collect_rows(token_grad, slot, n_seq, n_fsdp, size), ("seq", "fsdp"), 0, 0, tiled=True)


def embed_backward(token_grad, arrived, kept, height, after):
    n_seq, n_fsdp = lax.axis_size("seq"), lax.axis_size("fsdp")
    ids, owner, rank, slot, wanted, most, size = kept

    def plain(arrived, *after):
        total, squares = scatter_rows(arrived, wanted, height, after)
        return total, jnp.sum(squares)

    def rounds(arrived, *after):
        def another(carry):
            start, total = carry
            slot, rows = slot_lists(ids, owner, rank, start, size, n_fsdp, height)
            wanted = lax.all_to_all(
                jnp.concatenate([rows] * n_seq, axis=0), ("seq", "fsdp"), 0, 0, tiled=True
            )
            arrived = lax.all_to_all(
                collect_rows(token_grad, slot, n_seq, n_fsdp, size), ("seq", "fsdp"), 0, 0, tiled=True
            )
            return start + size, add_rows(total, arrived, wanted)

        total = plain(arrived, *after)[0]
        total = lax.while_loop(lambda carry: carry[0] <= most, another, (jnp.int32(size), total))[1]
        return total, jnp.sum(total * total)

    return lax.cond(most < size, plain, rounds, arrived, *after)


ANY = pl.BlockSpec(memory_space=pl.ANY)
HALF = KEY_VALUE_HEADS // 2


def turn(values):
    return pltpu.roll(values, HEAD_SIZE // 2, axis=1)


def columns(head):
    return slice(head * HEAD_SIZE, (head + 1) * HEAD_SIZE)


def shape_head(raw, cosine, sine, gain):
    raw = raw.astype(jnp.float32)
    scale = lax.rsqrt(jnp.mean(raw * raw, axis=-1, keepdims=True) + NORM_EPS)
    normed = raw * scale * gain
    return (normed * cosine + turn(normed) * sine).astype(jnp.bfloat16)


def shape_head_back(raw, cosine, sine, gain, grad):
    raw = raw.astype(jnp.float32)
    scale = lax.rsqrt(jnp.mean(raw * raw, axis=-1, keepdims=True) + NORM_EPS)
    grad = grad * cosine + turn(grad * sine)
    unit = raw * scale
    gain_grad = jnp.sum(grad * unit, axis=0, keepdims=True)
    grad = grad * gain
    inner = jnp.mean(grad * unit, axis=-1, keepdims=True)
    return (scale * (grad - unit * inner)).astype(jnp.bfloat16), gain_grad


def queries_kernel(raw_ref, cos_ref, sin_ref, gain_ref, out_ref):
    for head in range(QUERY_HEADS):
        at = columns(head)
        out_ref[:, at] = shape_head(raw_ref[:, at], cos_ref[...], sin_ref[...], gain_ref[0:1, :])


def keys_kernel(raw_ref, cos_ref, sin_ref, gain_ref, *out_refs):
    for head in range(KEY_VALUE_HEADS):
        out_ref = out_refs[head // HALF]
        out_ref[:, columns(head % HALF)] = shape_head(
            raw_ref[:, columns(head)], cos_ref[...], sin_ref[...], gain_ref[1:2, :]
        )
    for half in range(2):
        first = KEY_COLS + half * HALF * HEAD_SIZE
        out_refs[half][:, HALF * HEAD_SIZE :] = raw_ref[:, first : first + HALF * HEAD_SIZE]


def token_blocks(rows, width):
    return pl.BlockSpec((rows, width), lambda i: (i, 0))


def shape_queries(raw, cosine, sine, gains):
    tokens = raw.shape[0]
    rows = min(256, tokens)
    return pl.pallas_call(
        queries_kernel,
        grid=(tokens // rows,),
        in_specs=[
            token_blocks(rows, QUERY_COLS),
            token_blocks(rows, HEAD_SIZE),
            token_blocks(rows, HEAD_SIZE),
            pl.BlockSpec((2, HEAD_SIZE), lambda i: (0, 0)),
        ],
        out_specs=token_blocks(rows, QUERY_COLS),
        out_shape=jax.ShapeDtypeStruct((tokens, QUERY_COLS), jnp.bfloat16),
        compiler_params=pltpu.CompilerParams(vmem_limit_bytes=VMEM_BYTES),
        cost_estimate=pl.CostEstimate(flops=4 * 10**9, bytes_accessed=8 * 2**20, transcendentals=0),
    )(raw, cosine, sine, gains)


def shape_keys(raw, cosine, sine, gains):
    tokens = raw.shape[0]
    rows = min(256, tokens)
    half = jax.ShapeDtypeStruct((tokens, KEY_COLS), jnp.bfloat16)
    return pl.pallas_call(
        keys_kernel,
        grid=(tokens // rows,),
        in_specs=[
            token_blocks(rows, 2 * KEY_COLS),
            token_blocks(rows, HEAD_SIZE),
            token_blocks(rows, HEAD_SIZE),
            pl.BlockSpec((2, HEAD_SIZE), lambda i: (0, 0)),
        ],
        out_specs=[token_blocks(rows, KEY_COLS)] * 2,
        out_shape=[half, half],
        compiler_params=pltpu.CompilerParams(vmem_limit_bytes=VMEM_BYTES),
        cost_estimate=pl.CostEstimate(flops=2 * 10**9, bytes_accessed=8 * 2**20, transcendentals=0),
    )(raw, cosine, sine, gains)


def add_gain_grad(gain_ref, total):
    @pl.when(pl.program_id(0) == 0)
    def _():
        gain_ref[...] = jnp.zeros_like(gain_ref)

    gain_ref[0:1, :] += total


def queries_back_kernel(raw_ref, cos_ref, sin_ref, gain_ref, dq_ref, *refs):
    out_ref, dgain_ref = refs[-2:]
    total = jnp.zeros((1, HEAD_SIZE), jnp.float32)
    for head in range(QUERY_HEADS):
        at = columns(head)
        grad = dq_ref[:, at].astype(jnp.float32)
        out_ref[:, at], part = shape_head_back(raw_ref[:, at], cos_ref[...], sin_ref[...], gain_ref[0:1, :], grad)
        total = total + part
    add_gain_grad(dgain_ref, total)


def keys_back_kernel(raw_ref, cos_ref, sin_ref, gain_ref, own_a_ref, own_b_ref, more_a_ref, more_b_ref, *refs):
    out_ref, dgain_ref = refs[-2:]
    total = jnp.zeros((1, HEAD_SIZE), jnp.float32)
    for head in range(KEY_VALUE_HEADS):
        own_ref, more_ref = ((own_a_ref, more_a_ref), (own_b_ref, more_b_ref))[head // HALF]
        at, part_at = columns(head), columns(head % HALF)
        grad = own_ref[0, :, part_at] + more_ref[0, :, part_at].astype(jnp.float32)
        out_ref[:, at], part = shape_head_back(raw_ref[:, at], cos_ref[...], sin_ref[...], gain_ref[1:2, :], grad)
        total = total + part
    for half, (own_ref, more_ref) in enumerate(((own_a_ref, more_a_ref), (own_b_ref, more_b_ref))):
        first = KEY_COLS + half * HALF * HEAD_SIZE
        out_ref[:, first : first + HALF * HEAD_SIZE] = (
            own_ref[1] + more_ref[1].astype(jnp.float32)
        ).astype(jnp.bfloat16)
    add_gain_grad(dgain_ref, total)


def shape_back(kernel, raw, cosine, sine, gains, grads, after=()):
    tokens = raw.shape[0]
    rows = min(128, tokens)
    wide = [
        pl.BlockSpec((2, rows, g.shape[2]), lambda i: (0, i, 0)) if g.ndim == 3 else token_blocks(rows, g.shape[1])
        for g in grads
    ]
    return pl.pallas_call(
        kernel,
        grid=(tokens // rows,),
        in_specs=[
            token_blocks(rows, raw.shape[1]),
            token_blocks(rows, HEAD_SIZE),
            token_blocks(rows, HEAD_SIZE),
            pl.BlockSpec((2, HEAD_SIZE), lambda i: (0, 0)),
        ]
        + wide
        + [ANY] * len(after),
        out_specs=[token_blocks(rows, raw.shape[1]), pl.BlockSpec((8, HEAD_SIZE), lambda i: (0, 0))],
        out_shape=[
            jax.ShapeDtypeStruct(raw.shape, jnp.bfloat16),
            jax.ShapeDtypeStruct((8, HEAD_SIZE), jnp.float32),
        ],
        compiler_params=pltpu.CompilerParams(vmem_limit_bytes=VMEM_BYTES),
        cost_estimate=pl.CostEstimate(flops=5 * 10**9, bytes_accessed=20 * 2**20, transcendentals=0),
    )(raw, cosine, sine, gains, *grads, *after)


def both_heads(block):
    return jnp.concatenate([block[:, :HEAD_SIZE], block[:, HEAD_SIZE:]], axis=0)


def key_ranges(scalar_ref, step, rows, keys):
    first_own, first_before, low = scalar_ref[0], scalar_ref[1], scalar_ref[2 + 2 * step]
    before = (jnp.minimum(low, first_own) - first_before) // keys, (first_own - first_before) // keys
    own = jnp.maximum(low - first_own, 0) // keys, ((step + 1) * rows - 1) // keys + 1
    return first_own, first_before, before, own


def allowed_keys(begin_ref, offset, rows, keys):
    begin = begin_ref[...] - offset
    at = lax.broadcasted_iota(jnp.int32, (rows, 1), 0)
    key_at = lax.broadcasted_iota(jnp.int32, (rows, keys), 1)
    return begin, at, key_at


def visit_blocks(scalar_ref, begin_ref, rows, keys, refs, work):
    step = pl.program_id(1)
    first_own, first_before, before, own = key_ranges(scalar_ref, step, rows, keys)
    first_row = first_own + step * rows
    last_begin = scalar_ref[3 + 2 * step]

    def run(bounds, base, group):
        def one(j, carry):
            at = pl.ds(pl.multiple_of(j * keys, keys), keys)
            first_key = base + j * keys
            whole = (first_key + keys - 1 <= first_row) & (first_key >= last_begin)

            @pl.when(whole)
            def _():
                work(*group, at, None)

            @pl.when(jnp.logical_not(whole))
            def _():
                begin = begin_ref[...] - first_key
                row = (first_row - first_key) + lax.broadcasted_iota(jnp.int32, (rows, 1), 0)
                key = lax.broadcasted_iota(jnp.int32, (rows, keys), 1)
                work(*group, at, (key <= row) & (key >= begin))

            return carry

        lax.fori_loop(bounds[0], bounds[1], one, 0)

    run(before, first_before, refs[0])
    run(own, first_own, refs[1])


def forward_kernel(keys, scalar_ref, q_ref, kb_ref, vb_ref, k_ref, v_ref, begin_ref, *refs):
    o_ref, lse_ref, acc_ref = refs[-3:]
    rows = q_ref.shape[0]
    query = both_heads(q_ref[...])
    acc_ref[...] = jnp.zeros_like(acc_ref)
    ones = jnp.ones((keys, HEAD_SIZE), jnp.bfloat16)

    def work(key_ref, value_ref, at, mask):
        value = jnp.concatenate([value_ref[at, :], ones], axis=1)
        scores = [
            lax.dot_general(
                query[h * rows : (h + 1) * rows], key_ref[at, :], (((1,), (1,)), ((), ())),
                preferred_element_type=jnp.float32,
            )
            for h in range(2)
        ]
        for h in range(2):
            weight = jnp.exp2(scores[h] * (LOG2E * HEAD_SIZE**-0.5))
            if mask is not None:
                weight = jnp.where(mask, weight, 0.0)
            acc_ref[h * rows : (h + 1) * rows, :] += jnp.dot(
                weight.astype(jnp.bfloat16), value, preferred_element_type=jnp.float32
            )

    visit_blocks(scalar_ref, begin_ref, rows, keys, ((kb_ref, vb_ref), (k_ref, v_ref)), work)
    acc = acc_ref[...]
    total = acc[:, HEAD_SIZE : HEAD_SIZE + 1]
    out = (acc[:, :HEAD_SIZE] / total).astype(jnp.bfloat16)
    o_ref[:, :HEAD_SIZE] = out[:rows]
    o_ref[:, HEAD_SIZE:] = out[rows:]
    lse = jnp.log2(total)
    lse_ref[0, :, 0:1] = lse[:rows]
    lse_ref[0, :, 1:2] = lse[rows:]


def attention_specs(tokens, length, rows, first):
    key = lambda h, i, s: (0, h)
    value = lambda h, i, s: (0, HALF + h)
    return [
        pl.BlockSpec((rows, 2 * HEAD_SIZE), lambda h, i, s: (i, first + h)),
        pl.BlockSpec((length, HEAD_SIZE), key),
        pl.BlockSpec((length, HEAD_SIZE), value),
        pl.BlockSpec((tokens, HEAD_SIZE), key),
        pl.BlockSpec((tokens, HEAD_SIZE), value),
        pl.BlockSpec((rows, 1), lambda h, i, s: (i, 0)),
    ]


def attention_forward(scalars, query, before, own, begin, rows, keys, first, filled):
    tokens = query.shape[0]
    specs = attention_specs(tokens, before.shape[0], rows, first)
    return pl.pallas_call(
        functools.partial(forward_kernel, keys),
        grid_spec=pltpu.PrefetchScalarGridSpec(
            num_scalar_prefetch=1,
            grid=(HALF, tokens // rows),
            in_specs=specs + [ANY] * len(filled),
            out_specs=[specs[0], pl.BlockSpec((1, rows, 2), lambda h, i, s: (first + h, i, 0))],
            scratch_shapes=[pltpu.VMEM((2 * rows, 2 * HEAD_SIZE), jnp.float32)],
        ),
        out_shape=[
            jax.ShapeDtypeStruct((tokens, QUERY_COLS), jnp.bfloat16),
            jax.ShapeDtypeStruct((KEY_VALUE_HEADS, tokens, 2), jnp.float32),
        ],
        input_output_aliases={7 + i: i for i in range(len(filled))},
        compiler_params=pltpu.CompilerParams(vmem_limit_bytes=VMEM_BYTES),
        cost_estimate=pl.CostEstimate(flops=20 * 10**9, bytes_accessed=16 * 2**20, transcendentals=10**7),
    )(scalars, query, before, before, own, own, begin, *filled)


def backward_kernel(keys, scalar_ref, q_ref, kb_ref, vb_ref, k_ref, v_ref, begin_ref, do_ref, o_ref, lse_ref, *refs):
    dq_ref, before_ref, own_ref, acc_ref, dq_acc_ref = refs[-5:]
    step = pl.program_id(1)
    rows = q_ref.shape[0]
    query = both_heads(q_ref[...])
    grad = both_heads(do_ref[...])
    out = both_heads(o_ref[...])
    lse = jnp.concatenate([lse_ref[0, :, 0:1], lse_ref[0, :, 1:2]], axis=0)
    inner = jnp.sum(grad.astype(jnp.float32) * out.astype(jnp.float32), axis=-1, keepdims=True)

    @pl.when(step == 0)
    def _():
        acc_ref[...] = jnp.zeros_like(acc_ref)
        own_ref[...] = jnp.zeros_like(own_ref)

    dq_acc_ref[...] = jnp.zeros_like(dq_acc_ref)

    def work(key_ref, value_ref, sum_ref, at, mask):
        key = key_ref[at, :]
        score = lax.dot_general(query, key, (((1,), (1,)), ((), ())), preferred_element_type=jnp.float32)
        prob_grad = lax.dot_general(
            grad, value_ref[at, :], (((1,), (1,)), ((), ())), preferred_element_type=jnp.float32
        )
        prob = jnp.exp2(score * (LOG2E * HEAD_SIZE**-0.5) - lse)
        if mask is not None:
            prob = jnp.where(jnp.concatenate([mask, mask], axis=0), prob, 0.0)
        sum_ref[1, at, :] += lax.dot_general(
            prob.astype(jnp.bfloat16), grad, (((0,), (0,)), ((), ())), preferred_element_type=jnp.float32
        )
        score_grad = (prob * (prob_grad - inner)).astype(jnp.bfloat16)
        sum_ref[0, at, :] += lax.dot_general(
            score_grad, query, (((0,), (0,)), ((), ())), preferred_element_type=jnp.float32
        )
        dq_acc_ref[...] += jnp.dot(score_grad, key, preferred_element_type=jnp.float32)

    visit_blocks(
        scalar_ref, begin_ref, rows, keys, ((kb_ref, vb_ref, acc_ref), (k_ref, v_ref, own_ref)), work
    )
    dq = dq_acc_ref[...] * HEAD_SIZE**-0.5
    dq_ref[:, :HEAD_SIZE] = dq[:rows]
    dq_ref[:, HEAD_SIZE:] = dq[rows:]

    @pl.when(step == pl.num_programs(1) - 1)
    def _():
        own_ref[0] = own_ref[0] * HEAD_SIZE**-0.5
        before_ref[0] = (acc_ref[0] * HEAD_SIZE**-0.5).astype(before_ref.dtype)
        before_ref[1] = acc_ref[1].astype(before_ref.dtype)


def attention_backward(scalars, query, before, own, begin, grad_out, out, lse, rows, keys, first, filled, after):
    tokens, length = query.shape[0], before.shape[0]
    specs = attention_specs(tokens, length, rows, first)
    both = lambda h, i, s: (0, 0, h)
    before_type = jnp.bfloat16 if length == tokens else jnp.float32
    return pl.pallas_call(
        functools.partial(backward_kernel, keys),
        grid_spec=pltpu.PrefetchScalarGridSpec(
            num_scalar_prefetch=1,
            grid=(HALF, tokens // rows),
            in_specs=specs
            + [specs[0], specs[0], pl.BlockSpec((1, rows, 2), lambda h, i, s: (first + h, i, 0))]
            + [ANY] * (len(filled) + len(after)),
            out_specs=[
                specs[0],
                pl.BlockSpec((2, length, HEAD_SIZE), both),
                pl.BlockSpec((2, tokens, HEAD_SIZE), both),
            ],
            scratch_shapes=[
                pltpu.VMEM((2, length, HEAD_SIZE), jnp.float32),
                pltpu.VMEM((2 * rows, HEAD_SIZE), jnp.float32),
            ],
        ),
        out_shape=[
            jax.ShapeDtypeStruct((tokens, QUERY_COLS), jnp.float32),
            jax.ShapeDtypeStruct((2, length, HALF * HEAD_SIZE), before_type),
            jax.ShapeDtypeStruct((2, tokens, HALF * HEAD_SIZE), jnp.float32),
        ],
        input_output_aliases={10 + i: i for i in range(len(filled))},
        compiler_params=pltpu.CompilerParams(vmem_limit_bytes=VMEM_BYTES),
        cost_estimate=pl.CostEstimate(flops=40 * 10**9, bytes_accessed=40 * 2**20, transcendentals=10**7),
    )(scalars, query, before, before, own, own, begin, grad_out, out, lse, *filled, *after)


def tokens_before(own):
    if lax.axis_size("seq") != 2:
        return lax.all_gather(own, "seq", axis=0, tiled=True)
    return lax.ppermute(own, "seq", [(0, 1), (1, 0)])


def to_tokens_before(parts):
    if lax.axis_size("seq") != 2:
        return lax.psum_scatter(parts, "seq", scatter_dimension=1, tiled=True)
    return lax.ppermute(parts, "seq", [(0, 1), (1, 0)])


def fetch(weight):
    return lax.all_gather(weight.astype(jnp.bfloat16), ("seq", "fsdp"), axis=0, tiled=True)


def trade(values, axis, bit):
    count = lax.axis_size(axis)
    return lax.ppermute(values, axis, [(i, i ^ bit) for i in range(count)])


def halves(values, dim, at):
    return (
        lax.dynamic_index_in_dim(values, at, dim, keepdims=False),
        lax.dynamic_index_in_dim(values, 1 - at, dim, keepdims=False),
    )


def by_stages():
    return (lax.axis_size("seq"), lax.axis_size("fsdp")) == (2, 16)


def where_am_i():
    at = lax.axis_index("fsdp")
    return lax.axis_index("seq"), at >> 2, (at >> 1) & 1, at & 1


def gradient_kernel(height, core_ref, left_ref, right_ref, *refs):
    keep_ref, send_ref, turned_ref = refs[-3:]

    @pl.when(pl.program_id(1) == 0)
    def _():
        turned_ref[...] = left_ref[...].T

    product = jnp.dot(turned_ref[...], right_ref[...], preferred_element_type=jnp.float32)
    even = core_ref[0] == 0
    for p in range(keep_ref.shape[0]):
        first = product[2 * p * height : (2 * p + 1) * height]
        second = product[(2 * p + 1) * height : (2 * p + 2) * height]
        keep_ref[p] = jnp.where(even, first, second).astype(jnp.bfloat16)
        send_ref[p] = jnp.where(even, second, first).astype(jnp.bfloat16)


def gradient_blocks(left, right, rows, place, packed_rows, filled):
    tokens, tall = left.shape
    height = tall // 32
    pairs = rows // (2 * height)
    out = jax.ShapeDtypeStruct((16, packed_rows, D), jnp.bfloat16)
    block = pl.BlockSpec((pairs, height, D), lambda i, j, s: (i, place(j), 0))
    return pl.pallas_call(
        functools.partial(gradient_kernel, height),
        grid_spec=pltpu.PrefetchScalarGridSpec(
            num_scalar_prefetch=1,
            grid=(tall // rows, right.shape[1] // D),
            in_specs=[
                pl.BlockSpec((tokens, rows), lambda i, j, s: (0, i)),
                pl.BlockSpec((tokens, D), lambda i, j, s: (0, j)),
            ]
            + [ANY] * len(filled),
            out_specs=[block, block],
            scratch_shapes=[pltpu.VMEM((rows, tokens), jnp.bfloat16)],
        ),
        out_shape=[out, out],
        input_output_aliases={3 + i: i for i in range(len(filled))},
        compiler_params=pltpu.CompilerParams(vmem_limit_bytes=VMEM_BYTES),
        cost_estimate=pl.CostEstimate(
            flops=2 * tokens * tall * right.shape[1], bytes_accessed=16 * 2**20, transcendentals=0
        ),
    )(where_am_i()[3].reshape(1), left, right, *filled)


def core_kernel(at_ref, keep_ref, got_ref, *refs):
    left_keep_ref, left_send_ref, right_keep_ref, right_send_ref = refs[-4:]
    y_other, x_other = pl.program_id(0), pl.program_id(1)
    total = keep_ref[0] + got_ref[0]
    left, right = total[:, : D // 2], total[:, D // 2 :]

    @pl.when(y_other == 0)
    def _():
        left_keep_ref[0, 0] = left

    @pl.when(y_other == 1)
    def _():
        left_send_ref[0, 0] = left

    @pl.when(x_other == 0)
    def _():
        right_keep_ref[0, 0] = right

    @pl.when(x_other == 1)
    def _():
        right_send_ref[0, 0] = right


def sum_core(keep, send, after=()):
    rows = keep.shape[1]
    got = trade(send, "fsdp", 1)
    y_at, _, x_at, _ = where_am_i()

    def chip(a, b, z, s):
        return (((a ^ s[0]) * 4 + z) * 2 + (b ^ s[1]), 0, 0)

    def left_keep(a, b, z, s):
        return (jnp.where(a == 0, z, 3), jnp.where(a == 0, b, 1) ^ s[1], 0, 0)

    def left_send(a, b, z, s):
        return (jnp.where(a == 1, z, 0), jnp.where(a == 1, b, 0) ^ s[1], 0, 0)

    def right_keep(a, b, z, s):
        return (a ^ s[0], jnp.where(b == 0, z, 3), 0, 0)

    def right_send(a, b, z, s):
        return (jnp.where(b == 1, a, 0) ^ s[0], jnp.where(b == 1, z, jnp.where(a == 0, 0, 3)), 0, 0)

    full = pl.BlockSpec((1, rows, D), chip)
    part = lambda index: pl.BlockSpec((1, 1, rows, D // 2), index)
    left = jax.ShapeDtypeStruct((4, 2, rows, D // 2), jnp.bfloat16)
    right = jax.ShapeDtypeStruct((2, 4, rows, D // 2), jnp.bfloat16)
    lk, ls, rk, rs = pl.pallas_call(
        core_kernel,
        grid_spec=pltpu.PrefetchScalarGridSpec(
            num_scalar_prefetch=1,
            grid=(2, 2, 4),
            in_specs=[full, full] + [ANY] * len(after),
            out_specs=[part(left_keep), part(left_send), part(right_keep), part(right_send)],
        ),
        out_shape=[left, left, right, right],
        compiler_params=pltpu.CompilerParams(vmem_limit_bytes=VMEM_BYTES),
        cost_estimate=pl.CostEstimate(flops=10**9, bytes_accessed=96 * 2**10 * rows, transcendentals=0),
    )(jnp.stack([y_at, x_at]), keep, got, *after)
    return (lk, rk), (ls, rs)


def sum_first(keep, send):
    y_at, _, x_at, _ = where_am_i()
    low, wide = jnp.bfloat16, jnp.float32
    left = keep[0].astype(wide) + trade(send[0], "seq", 1).astype(wide)
    right = keep[1].astype(wide) + trade(send[1], "fsdp", 2).astype(wide)
    left_keep, left_send = halves(left, 1, x_at)
    right_keep, right_send = halves(right, 0, y_at)
    return (left_keep, right_keep), (left_send.astype(low), right_send.astype(low))


def sum_second(keep, send):
    z_at = where_am_i()[1]
    left = keep[0] + trade(send[0], "fsdp", 2).astype(jnp.float32)
    right = keep[1] + trade(send[1], "seq", 1).astype(jnp.float32)
    total = jnp.concatenate([left, right], axis=-1)
    own = lax.dynamic_index_in_dim(total, z_at, 0, keepdims=False)
    sends = tuple(
        lax.dynamic_index_in_dim(total, z_at ^ other, 0, keepdims=False).astype(jnp.bfloat16) for other in (1, 2, 3)
    )
    return own, sends


def sum_last(keep, send):
    total = keep
    for other in (1, 2, 3):
        total = total + trade(send[other - 1], "fsdp", 4 * other).astype(jnp.float32)
    return total


def beside(total, height, starts):
    return jnp.concatenate([total[r : r + height] for r in starts], axis=1)


def plain_sum(left, right):
    grad = lax.dot_general(left, right, (((0,), (0,)), ((), ())), preferred_element_type=jnp.float32)
    return lax.psum_scatter(grad, ("seq", "fsdp"), scatter_dimension=0, tiled=True)


def activation_back_kernel(grad_ref, down_ref, gate_ref, up_ref, gate_grad_ref, up_grad_ref):
    grad = lax.dot_general(
        grad_ref[...], down_ref[...], (((1,), (1,)), ((), ())), preferred_element_type=jnp.float32
    )
    gate = gate_ref[...]
    share = 0.5 + 0.5 * jnp.tanh(0.5 * gate)
    silu = gate * share
    up_grad_ref[...] = (grad * silu).astype(jnp.bfloat16)
    gate_grad_ref[...] = (grad * up_ref[...] * (share + silu - silu * share)).astype(jnp.bfloat16)


def activation_back(grad, down, gate_up):
    tokens, width = gate_up.shape
    rows, wide = min(512, tokens), 512
    tiles = width // (2 * wide)
    out = jax.ShapeDtypeStruct((tokens, width // 2), jnp.bfloat16)
    block = pl.BlockSpec((rows, wide), lambda i, j: (i, j))
    return pl.pallas_call(
        activation_back_kernel,
        grid=(tokens // rows, tiles),
        in_specs=[
            pl.BlockSpec((rows, D), lambda i, j: (i, 0)),
            pl.BlockSpec((wide, D), lambda i, j: (j, 0)),
            block,
            pl.BlockSpec((rows, wide), lambda i, j: (i, tiles + j)),
        ],
        out_specs=[block, block],
        out_shape=[out, out],
        compiler_params=pltpu.CompilerParams(vmem_limit_bytes=VMEM_BYTES),
        cost_estimate=pl.CostEstimate(
            flops=tokens * width * D, bytes_accessed=6 * tokens * width, transcendentals=tokens * width // 2
        ),
    )(grad, down, gate_up, gate_up)


def adam_update(weight, moment_one, moment_two, grad, factor, step_float):
    grad = grad * factor
    moment_one = BETA_ONE * moment_one + (1.0 - BETA_ONE) * grad
    moment_two = BETA_TWO * moment_two + (1.0 - BETA_TWO) * grad * grad
    fix_one = 1.0 - BETA_ONE**step_float
    fix_two = 1.0 - BETA_TWO**step_float
    weight = weight - LEARN_RATE * (
        moment_one / fix_one / (jnp.sqrt(moment_two / fix_two) + ADAM_EPS) + WEIGHT_DECAY * weight
    )
    return (weight, moment_one, moment_two)


def body(
    token_ids,
    seq_lengths,
    pairing,
    step_count,
    embedding,
    embedding_one,
    embedding_two,
    qkv_weight,
    qkv_one,
    qkv_two,
    out_weight,
    out_one,
    out_two,
    gate_up_weight,
    gate_up_one,
    gate_up_two,
    down_weight,
    down_one,
    down_two,
    norm_gains,
    gains_one,
    gains_two,
    score_weight,
    score_one,
    score_two,
):
    seq_at = lax.axis_index("seq")
    group_at = lax.axis_index("fsdp")
    token_rows = token_ids.shape[1]
    per_group = seq_lengths.shape[1] - 1
    lengths = seq_lengths[0]
    bounds = jnp.stack([jnp.sum(lengths[: j + 1]) for j in range(per_group)])
    token_pos = seq_at * token_rows + jnp.arange(token_rows, dtype=jnp.int32)
    segment, begin = layout(bounds, token_pos)
    frequency = ROPE_THETA ** (
        -2.0 * jnp.arange(HEAD_SIZE // 2, dtype=jnp.float32) / HEAD_SIZE
    )
    angles = (token_pos - begin).astype(jnp.float32)[:, None] * frequency[None, :]
    cosine, sine = jnp.cos(angles), jnp.sin(angles)
    cosine = jnp.concatenate([cosine, cosine], axis=1)
    sine = jnp.concatenate([-sine, sine], axis=1)
    query_rows = min(512, token_rows)
    key_rows = min(512, token_rows)
    begin_column = begin[:, None]
    attn_gain = norm_gains[:D]
    mlp_gain = norm_gains[D : 2 * D]
    final_gain = norm_gains[2 * D : 3 * D]
    head_gains = norm_gains[3 * D :].reshape(2, HEAD_SIZE)
    first_own = seq_at * token_rows
    first_before = first_own - token_rows if lax.axis_size("seq") == 2 else 0 * first_own
    scalars = jnp.concatenate(
        [
            jnp.stack([first_own, first_before]),
            jnp.stack([begin[::query_rows], begin[query_rows - 1 :: query_rows]], axis=1).reshape(-1),
        ]
    )
    qkv_full = fetch(qkv_weight)
    out_full, gate_up_full, down_full = fetch(out_weight), fetch(gate_up_weight), fetch(down_weight)
    embedded, kept = embed_forward(token_ids, embedding)
    resid_in = embedded.astype(jnp.float32)
    normed_low = rms_norm(resid_in, attn_gain).astype(jnp.bfloat16)
    key_value_raw = jnp.dot(
        normed_low, qkv_full[:, QUERY_COLS:], preferred_element_type=jnp.float32
    ).astype(jnp.bfloat16)
    own_a, own_b = shape_keys(key_value_raw, cosine, sine, head_gains)
    before_a, before_b = tokens_before(own_a), tokens_before(own_b)
    query_raw = jnp.dot(
        normed_low, qkv_full[:, :QUERY_COLS], preferred_element_type=jnp.float32
    ).astype(jnp.bfloat16)
    query_low = shape_queries(query_raw, cosine, sine, head_gains)
    results = attention_forward(
        scalars, query_low, before_a, own_a, begin_column, query_rows, key_rows, 0, ()
    )
    merged, lse = attention_forward(
        scalars, query_low, before_b, own_b, begin_column, query_rows, key_rows, HALF, tuple(results)
    )
    resid_mid = resid_in + jnp.dot(merged, out_full, preferred_element_type=jnp.float32)
    normed_two = rms_norm(resid_mid, mlp_gain).astype(jnp.bfloat16)
    gate_up = jnp.dot(normed_two, gate_up_full, preferred_element_type=jnp.float32)
    activated = (jax.nn.silu(gate_up[:, :FF]) * gate_up[:, FF:]).astype(jnp.bfloat16)
    resid_out = resid_mid + jnp.dot(activated, down_full, preferred_element_type=jnp.float32)
    final = rms_norm(resid_out, final_gain)
    per_token = jnp.sum(final * score_weight, axis=1)
    slot_list = jnp.arange(per_group, dtype=jnp.int32)
    seq_size = seq_lengths[0, :per_group].astype(jnp.float32)
    picker = (segment[None, :] == slot_list[:, None]).astype(jnp.float32) / seq_size[:, None]
    own_scores = jnp.sum(picker * per_token[None, :], axis=1)
    seq_total = pairing.shape[0]
    score_board = lax.dynamic_update_slice(
        jnp.zeros((seq_total,), jnp.float32), own_scores, (group_at * per_group,)
    )
    all_scores = sum_small(score_board, 3)
    pair_table = pairing.reshape(-1, 2)
    seq_ids = jnp.arange(seq_total, dtype=jnp.int32)
    choose = (pair_table[:, 0:1] == seq_ids[None, :]).astype(jnp.float32)
    reject = (pair_table[:, 1:2] == seq_ids[None, :]).astype(jnp.float32)
    margin = jnp.sum((choose - reject) * all_scores[None, :], axis=1)
    ranking_loss = jnp.sum(jax.nn.softplus(-margin))
    margin_grad = -jax.nn.sigmoid(-margin)
    score_grads = jnp.sum(margin_grad[:, None] * (choose - reject), axis=0)
    own_grads = lax.dynamic_slice_in_dim(score_grads, group_at * per_group, per_group)
    token_grad = jnp.sum(own_grads[:, None] * picker, axis=0)
    score_part = jnp.sum(token_grad[:, None] * final, axis=0)
    final_grad = token_grad[:, None] * score_weight[None, :]
    final_back = jax.vjp(rms_norm, resid_out, final_gain)[1]
    dresid_out, dfinal_gain = final_back(final_grad)
    mlp_low = dresid_out.astype(jnp.bfloat16)
    staged = by_stages()
    keep, send = (), ()
    if staged:
        early = gradient_blocks(activated, mlp_low, 768, lambda j: 0, 288, ())
    else:
        down_shard = plain_sum(activated, mlp_low)
    gate_low, up_low = activation_back(mlp_low, down_full, gate_up)
    if staged:
        early = gradient_blocks(normed_two, gate_low, 512, lambda j: 3 + j, 288, tuple(early))
        early = gradient_blocks(normed_two, up_low, 512, lambda j: 6 + j, 288, tuple(early))
    else:
        gate_up_shard = jnp.concatenate([plain_sum(normed_two, gate_low), plain_sum(normed_two, up_low)], axis=1)
    normed_two_grad = jnp.dot(
        gate_low, gate_up_full[:, :FF].T, preferred_element_type=jnp.float32
    ) + jnp.dot(up_low, gate_up_full[:, FF:].T, preferred_element_type=jnp.float32)
    mid_back = jax.vjp(rms_norm, resid_mid, mlp_gain)[1]
    mid_extra, dmlp_gain = mid_back(normed_two_grad)
    dresid_mid = dresid_out + mid_extra
    attn_low = dresid_mid.astype(jnp.bfloat16)
    if staged:
        late = gradient_blocks(merged, attn_low, 512, lambda j: 0, 192, ())
        keep, send = sum_core(*early, (attn_low,))
    else:
        out_shard = plain_sum(merged, attn_low)
    merged_grad = jnp.dot(attn_low, out_full.T, preferred_element_type=jnp.float32).astype(
        jnp.bfloat16
    )
    common = (begin_column, merged_grad, merged, lse, query_rows, key_rows)
    query_grad, before_grad_a, own_grad_a = attention_backward(
        scalars, query_low, before_a, own_a, *common, 0, (), send
    )
    more_a = to_tokens_before(before_grad_a)
    if staged:
        keep, send = sum_first(keep, send)
    query_grad, before_grad_b, own_grad_b = attention_backward(
        scalars, query_low, before_b, own_b, *common, HALF, (query_grad,), send
    )
    more_b = to_tokens_before(before_grad_b)
    if staged:
        keep, send = sum_second(keep, send)
    query_raw_grad, query_sums = shape_back(
        queries_back_kernel, query_raw, cosine, sine, head_gains, (query_grad,), send
    )
    total = sum_last(keep, send) if staged else begin_column
    key_value_raw_grad, key_sums = shape_back(
        keys_back_kernel, key_value_raw, cosine, sine, head_gains, (own_grad_a, own_grad_b, more_a, more_b), (total,)
    )
    if staged:
        down_shard = total[:96]
        gate_up_shard = beside(total, 32, range(96, 288, 32))
        late = gradient_blocks(normed_low, query_raw_grad, 512, lambda j: 2 + j, 192, tuple(late))
        late = gradient_blocks(normed_low, key_value_raw_grad, 512, lambda j: 4 + j, 192, tuple(late))
        keep, send = sum_core(*late)
    else:
        send = ()
        qkv_shard = jnp.concatenate(
            [plain_sum(normed_low, query_raw_grad), plain_sum(normed_low, key_value_raw_grad)], axis=1
        )
    normed_grad = jnp.dot(
        query_raw_grad, qkv_full[:, :QUERY_COLS].T, preferred_element_type=jnp.float32
    ) + jnp.dot(key_value_raw_grad, qkv_full[:, QUERY_COLS:].T, preferred_element_type=jnp.float32)
    in_back = jax.vjp(rms_norm, resid_in, attn_gain)[1]
    in_extra, dattn_gain = in_back(normed_grad)
    dresid_in = dresid_mid + in_extra
    token_grad_low = dresid_in.astype(jnp.bfloat16)
    arrived = embed_send(token_grad_low, kept)
    if staged:
        keep, send = sum_first(keep, send)
        keep, send = sum_second(keep, send)
    embed_grad, square = embed_backward(token_grad_low, arrived, kept, embedding.shape[0], send)
    if staged:
        total = sum_last(keep, send)
        out_shard, qkv_shard = total[:64], beside(total, 32, range(64, 192, 32))
    shards = (qkv_shard, out_shard, gate_up_shard, down_shard)
    for shard in shards:
        square = square + jnp.sum(shard * shard)
    gain_part = jnp.concatenate([dattn_gain, dmlp_gain, dfinal_gain, query_sums[0], key_sums[0]])
    gain_count = gain_part.shape[0]
    sums = sum_small(jnp.concatenate([gain_part, score_part, square.reshape(1)]), 4)
    gain_sum, score_sum, square_sum = sums[:gain_count], sums[gain_count:-1], sums[-1]
    grad_norm = jnp.sqrt(square_sum + jnp.sum(gain_sum * gain_sum) + jnp.sum(score_sum * score_sum))
    factor = CLIP_NORM / jnp.maximum(grad_norm, CLIP_NORM)
    step_float = step_count[0]
    e_new = adam_update(embedding, embedding_one, embedding_two, embed_grad, factor, step_float)
    q_new = adam_update(qkv_weight, qkv_one, qkv_two, shards[0], factor, step_float)
    o_new = adam_update(out_weight, out_one, out_two, shards[1], factor, step_float)
    g_new = adam_update(gate_up_weight, gate_up_one, gate_up_two, shards[2], factor, step_float)
    d_new = adam_update(down_weight, down_one, down_two, shards[3], factor, step_float)
    n_new = adam_update(norm_gains, gains_one, gains_two, gain_sum, factor, step_float)
    s_new = adam_update(score_weight, score_one, score_two, score_sum, factor, step_float)
    clipped_gains = gain_sum * factor
    return (
        ranking_loss,
        grad_norm,
        e_new[0],
        e_new[1],
        e_new[2],
        q_new[0],
        q_new[1],
        q_new[2],
        o_new[0],
        o_new[1],
        o_new[2],
        g_new[0],
        g_new[1],
        g_new[2],
        d_new[0],
        d_new[1],
        d_new[2],
        clipped_gains,
        n_new[1],
        n_new[2],
        s_new[0],
        s_new[1],
        s_new[2],
    )


def solution(mesh):
    return jax.shard_map(
        body,
        mesh=mesh,
        in_specs=(
            P("fsdp", "seq"),
            P("fsdp", None),
            P(),
            P(),
            P("fsdp", "seq"),
            P("fsdp", "seq"),
            P("fsdp", "seq"),
            P(("seq", "fsdp"), None),
            P(("seq", "fsdp"), None),
            P(("seq", "fsdp"), None),
            P(("seq", "fsdp"), None),
            P(("seq", "fsdp"), None),
            P(("seq", "fsdp"), None),
            P(("seq", "fsdp"), None),
            P(("seq", "fsdp"), None),
            P(("seq", "fsdp"), None),
            P(("seq", "fsdp"), None),
            P(("seq", "fsdp"), None),
            P(("seq", "fsdp"), None),
            P(),
            P(),
            P(),
            P(),
            P(),
            P(),
        ),
        out_specs=(
            P(),
            P(),
            P("fsdp", "seq"),
            P("fsdp", "seq"),
            P("fsdp", "seq"),
            P(("seq", "fsdp"), None),
            P(("seq", "fsdp"), None),
            P(("seq", "fsdp"), None),
            P(("seq", "fsdp"), None),
            P(("seq", "fsdp"), None),
            P(("seq", "fsdp"), None),
            P(("seq", "fsdp"), None),
            P(("seq", "fsdp"), None),
            P(("seq", "fsdp"), None),
            P(("seq", "fsdp"), None),
            P(("seq", "fsdp"), None),
            P(("seq", "fsdp"), None),
            P(),
            P(),
            P(),
            P(),
            P(),
            P(),
        ),
        check_vma=False,
    )
```
